32 devices in a mesh: groups: 2 (over y), lat: 4 (over z), mesh: 2 (over x), feat: 2 (over core).
Axes of the slice: x: 2, y: 2, z: 4, core: 2. Of those that a mesh axis runs over, the one named last changes fastest.
Arguments:
- grid_in: bfloat16 [8192, 512], P(('groups', 'lat', 'mesh'), 'feat'), parts along dimension 0, may hold values from -6 to 6
- mesh_in: bfloat16 [2048, 512], P(('groups', 'mesh'), 'feat'), parts along dimension 0, may hold values from -6 to 6
- w_enc: bfloat16 [512, 512], P(None, 'feat'), may hold values from -0.25 to 0.25
- w_proc: bfloat16 [512, 512], P(None, 'feat'), may hold values from -0.25 to 0.25
- w_dec: bfloat16 [512, 512], P(None, 'feat'), may hold values from -0.25 to 0.25
- enc_dst: int32 [8192, 4], P(('groups', 'lat', 'mesh')), parts along dimension 0, may hold values from 0 to 1023, as said below
- enc_count: int32 [8192], P(('groups', 'lat', 'mesh')), parts along dimension 0, may hold values from 1 to 4
- dec_src: int32 [8192, 3], P(('groups', 'lat', 'mesh')), parts along dimension 0, may hold values from 0 to 1023, as said below
- proc_src: int32 [2048, 6], P(('groups', 'mesh')), parts along dimension 0, may hold values from 0 to 1023
- cotangent: bfloat16 [8192, 512], P(('groups', 'lat', 'mesh'), 'feat'), parts along dimension 0, may hold values from -1.5 to 1.5
Outputs:
- grad_grid: bfloat16 [8192, 512], P(('groups', 'lat', 'mesh'), 'feat'), parts along dimension 0
- grad_mesh: bfloat16 [2048, 512], P(('groups', 'mesh'), 'feat'), parts along dimension 0
- grad_w_enc: float32 [1024, 512], P('groups', 'feat'), parts along dimension 0
- grad_w_proc: float32 [1024, 512], P('groups', 'feat'), parts along dimension 0
- grad_w_dec: float32 [1024, 512], P('groups', 'feat'), parts along dimension 0
The draws below stay inside these ranges and needn't reach their ends.
There are 2 independent parts, one for each index of `groups`. The reference program is written for one: setup_inputs(seed, part) draws one part's arguments, and reference() takes and returns one part's arrays. A program takes and returns all parts, laid end to end along the dimension named above; an argument that names none is the same for every part. Nothing has to cross between parts.
Inputs may be any that keep to these rules, and one draw needn't show every extreme that they name: `enc_dst`: number the latitude homes h = l * 2 + m for l < 4, m < 2; home h holds mesh nodes m * 512 + l * 128 + j for j < 128. Grid node g lies in band b = g // 512, and each of its encoder slots names a node of home b - 1, b or b + 1. `dec_src`: each source of grid node g names a node of home b - 1, b or b + 1, with homes and bands numbered as for enc_dst.
All inputs are finite; a program needn't handle non-finite values.
Results may differ from the reference program's by a relative error of at most 0.019.
Values may be sent and summed in bfloat16 or wider, within the bound.
A program may use at most 64 MiB of HBM per device.

```python
import jax
import jax.numpy as jnp
from jax import lax

L = 512
G_DEV = 512
M_DEV = 512
KE = 4
KD = 3
KP = 6
HOME = 128
G = 4096
M = 1024
N_LAT = 4
N_MESH = 2
N_FEAT = 2


def window_nodes(key, slot_count):
    key_home, key_inner = jax.random.split(key)
    total_rows = G_DEV * N_LAT * N_MESH
    band_index = (jnp.arange(total_rows, dtype=jnp.int32) // G_DEV)[:, None]
    offset = jax.random.randint(key_home, (total_rows, slot_count), -1, 2, dtype=jnp.int32)
    home_id = jnp.clip(band_index + offset, 0, N_LAT * N_MESH - 1)
    inner_row = jax.random.randint(key_inner, (total_rows, slot_count), 0, HOME, dtype=jnp.int32)
    node = home_id % N_MESH * M_DEV + home_id // N_MESH * HOME + inner_row
    return node.astype(jnp.int32)


def draw_enc_dst(key, part):
    key = jax.random.fold_in(key, 11)
    return window_nodes(key, KE)


def draw_dec_src(key, part):
    key = jax.random.fold_in(key, 23)
    return window_nodes(key, KD)


def with_ends(entries, rng, least, top_value):
    longest = entries.shape.index(max(entries.shape))
    spots = []
    for shift in (0, 1):
        where = [jax.random.randint(jax.random.fold_in(rng, axis), (), 0, length) for axis, length in enumerate(entries.shape)]
        where[longest] = (where[longest] + shift) % entries.shape[longest]
        spots.append(tuple(where))
    return entries.at[spots[0]].set(least).at[spots[1]].set(top_value)


def block_levels(stream_key, shape, shards, least, largest):
    loudness, own = 1.0, jax.random.fold_in(stream_key, 6)
    for axis_at, blocks in shards:
        draws = jnp.exp(jax.random.uniform(jax.random.fold_in(own, axis_at), (blocks,), jnp.float32, least / len(shards), largest / len(shards)))
        loudness = loudness * jnp.repeat(draws, shape[axis_at] // blocks).reshape([-1 if axis == axis_at else 1 for axis in range(len(shape))])
    return loudness


def bell_draw(stream_key, dims, width, most, pieces=(), kind=jnp.bfloat16):
    loudness = block_levels(stream_key, dims, pieces, -0.22, 0.18) if pieces else 1.0
    result = jax.random.normal(stream_key, dims, jnp.float32) * width * loudness
    return jnp.minimum(jnp.maximum(result, -most), most).astype(kind)


def setup_inputs(seed: int = 0, part: int = 0) -> dict:
    arg_keys = jax.random.split(jax.random.key(seed), 11)
    own_keys = jax.random.split(jax.random.fold_in(arg_keys[10], part), 11)
    return {
        "grid_in": bell_draw(own_keys[0], (G, L), 1.0, 6.0, ((0, 8), (1, 2))),
        "mesh_in": bell_draw(own_keys[1], (M, L), 1.0, 6.0, ((0, 2), (1, 2))),
        "w_enc": bell_draw(arg_keys[2], (L, L), L ** -0.5, 0.25, ((1, 2),)),
        "w_proc": bell_draw(arg_keys[3], (L, L), L ** -0.5, 0.25, ((1, 2),)),
        "w_dec": bell_draw(arg_keys[4], (L, L), L ** -0.5, 0.25, ((1, 2),)),
        "enc_dst": draw_enc_dst(jax.random.fold_in(jax.random.fold_in(arg_keys[10], part), 71), part),
        "enc_count": with_ends(jax.random.randint(own_keys[6], (G,), 1, KE + 1), jax.random.fold_in(own_keys[6], 1), 1, KE).astype(jnp.int32),
        "dec_src": draw_dec_src(jax.random.fold_in(jax.random.fold_in(arg_keys[10], part), 71), part),
        "proc_src": with_ends(jax.random.randint(own_keys[8], (M, KP), 0, M), jax.random.fold_in(own_keys[8], 1), 0, M - 1).astype(jnp.int32),
        "cotangent": bell_draw(own_keys[9], (G, L), 0.25, 1.5, ((0, 8), (1, 2))),
    }


def silu_grad(pre):
    sig = jax.nn.sigmoid(pre)
    return sig * (1.0 + pre * (1.0 - sig))

def width_back(d_pre, weight):
    part_cols = L // N_FEAT
    summed = jnp.zeros((d_pre.shape[0], L), jnp.float32)
    for which in range(N_FEAT):
        lo_col = which * part_cols
        part = jnp.dot(d_pre[:, lo_col:lo_col + part_cols], weight[:, lo_col:lo_col + part_cols].T, preferred_element_type=jnp.float32)
        part = lax.optimization_barrier(part.astype(jnp.bfloat16))
        summed = summed + part.astype(jnp.float32)
    return summed

def reference(grid_in, mesh_in, w_enc, w_proc, w_dec, enc_dst, enc_count, dec_src, proc_src, cotangent):
    enc_factor = HOME / G_DEV
    pre_enc = jnp.dot(grid_in, w_enc, preferred_element_type=jnp.float32)
    enc_msg = jax.nn.silu(pre_enc).astype(jnp.bfloat16)
    is_valid = jnp.arange(KE, dtype=jnp.int32)[None, :] < enc_count[:, None]
    aggregate = jnp.zeros((M, L), jnp.float32)
    for column in range(KE):
        masked = jnp.where(is_valid[:, column, None], enc_msg.astype(jnp.float32), jnp.float32(0.0))
        aggregate = aggregate.at[enc_dst[:, column]].add(masked)
    aggregate = aggregate * enc_factor
    latent_one = (mesh_in.astype(jnp.float32) + aggregate).astype(jnp.bfloat16)
    pre_proc = jnp.dot(latent_one, w_proc, preferred_element_type=jnp.float32)
    proc_msg = jax.nn.silu(pre_proc).astype(jnp.bfloat16)
    neighbour_sum = jnp.zeros((M, L), jnp.float32)
    for column in range(KP):
        neighbour_sum = neighbour_sum + proc_msg[proc_src[:, column]].astype(jnp.float32)
    latent_two = (latent_one.astype(jnp.float32) + neighbour_sum / KP).astype(jnp.bfloat16)
    pre_dec = jnp.dot(latent_two, w_dec, preferred_element_type=jnp.float32)
    cot_wide = cotangent.astype(jnp.float32)
    d_dec = jnp.zeros((M, L), jnp.float32)
    for column in range(KD):
        d_dec = d_dec.at[dec_src[:, column]].add(cot_wide)
    d_dec = (d_dec / KD).astype(jnp.bfloat16)
    d_pre_dec = (d_dec.astype(jnp.float32) * silu_grad(pre_dec)).astype(jnp.bfloat16)
    grad_w_dec = jnp.dot(latent_two.T, d_pre_dec, preferred_element_type=jnp.float32)
    d_two = width_back(d_pre_dec, w_dec)
    d_two_b = d_two.astype(jnp.bfloat16)
    d_proc = jnp.zeros((M, L), jnp.float32)
    for column in range(KP):
        d_proc = d_proc.at[proc_src[:, column]].add(d_two_b.astype(jnp.float32))
    d_proc = d_proc / KP
    d_pre_proc = (d_proc * silu_grad(pre_proc)).astype(jnp.bfloat16)
    grad_w_proc = jnp.dot(latent_one.T, d_pre_proc, preferred_element_type=jnp.float32)
    d_one = d_two + width_back(d_pre_proc, w_proc)
    grad_mesh = d_one.astype(jnp.bfloat16)
    d_enc = jnp.zeros((G, L), jnp.float32)
    for column in range(KE):
        picked = grad_mesh[enc_dst[:, column]].astype(jnp.float32)
        d_enc = d_enc + jnp.where(is_valid[:, column, None], picked, jnp.float32(0.0))
    d_enc = d_enc * enc_factor
    d_pre_enc = (d_enc * silu_grad(pre_enc)).astype(jnp.bfloat16)
    grad_w_enc = jnp.dot(grid_in.T, d_pre_enc, preferred_element_type=jnp.float32)
    grad_grid = (cot_wide + width_back(d_pre_enc, w_enc)).astype(jnp.bfloat16)
    return (grad_grid, grad_mesh, grad_w_enc, grad_w_proc, grad_w_dec)
```

```python
import functools

import jax
import jax.numpy as jnp
from jax import lax
from jax.experimental import pallas as pl
from jax.experimental.pallas import tpu as pltpu
from jax.sharding import PartitionSpec as P

KE = 4
KD = 3
KP = 6


def with_halo(value, sides, width):
    for axis, dim in sides:
        size, length = (lax.axis_size(axis), value.shape[dim])
        up = [(i, (i + 1) % size) for i in range(size - 1)]
        down = [(j, i) for i, j in up]
        last = lax.slice_in_dim(value, length - width, length, axis=dim)
        first = lax.slice_in_dim(value, 0, width, axis=dim)
        before = lax.ppermute(last, axis, up)
        after = lax.ppermute(first, axis, down)
        value = jnp.concatenate([before, value, after], axis=dim)
    return value


def silu_grad(pre):
    sig = jax.nn.sigmoid(pre)
    return sig * (1.0 + pre * (1.0 - sig))


def window_slots(targets, is_valid, shard_rows, home_rows, n_mesh, band_index):
    owner_shard = targets // shard_rows
    inner_row = targets % shard_rows
    home_id = inner_row // home_rows * n_mesh + owner_shard
    slot_ids = (home_id - band_index + 1) * home_rows + inner_row % home_rows
    return jnp.where(is_valid, slot_ids, -1)


def window_matrix(slot_ids, win_rows):
    row_ids = jnp.arange(win_rows, dtype=jnp.int32)[:, None]
    matrix = jnp.zeros((win_rows, slot_ids.shape[0]), jnp.bfloat16)
    for column in range(slot_ids.shape[1]):
        matrix = matrix + (row_ids == slot_ids[:, column][None, :]).astype(jnp.bfloat16)
    return matrix


def band_sum(window, home_rows):
    stacked = window.reshape(3, home_rows, window.shape[1])
    padded_win = with_halo(stacked.astype(jnp.bfloat16), ((("lat", "mesh"), 0),), 3).astype(
        stacked.dtype
    )
    return padded_win[2] + padded_win[4] + padded_win[6]


def collect_rows(home_block):
    return lax.all_gather(home_block, "lat", axis=0, tiled=True)


def widen(latent):
    return lax.all_gather(latent, "feat", axis=1, tiled=True)


def back_product(d_pre, weight):
    return lax.dot_general(
        d_pre, weight, (((1,), (1,)), ((), ())), preferred_element_type=jnp.float32
    )


def mesh_back(d_pre, weight):
    return lax.psum_scatter(
        back_product(d_pre, weight).astype(jnp.bfloat16), "feat", scatter_dimension=1, tiled=True
    ).astype(jnp.float32)


def contract_rows(left_rows, right_rows):
    return lax.dot_general(
        left_rows, right_rows, (((0,), (0,)), ((), ())), preferred_element_type=jnp.float32
    )


def local_staged(grid_in, mesh_in, w_enc, w_proc, w_dec, enc_dst, enc_count, dec_src, proc_src, cotangent):
    n_mesh = lax.axis_size("mesh")
    n_lat = lax.axis_size("lat")
    shard_rows = mesh_in.shape[0]
    home_rows = shard_rows // n_lat
    grid_rows = grid_in.shape[0]
    enc_factor = home_rows / grid_rows
    band_index = lax.axis_index("lat") * n_mesh + lax.axis_index("mesh")
    home_first = lax.axis_index("lat") * home_rows
    win_rows = 3 * home_rows
    enc_valid = jnp.arange(KE, dtype=jnp.int32)[None, :] < enc_count[:, None]
    enc_matrix = window_matrix(
        window_slots(enc_dst, enc_valid, shard_rows, home_rows, n_mesh, band_index), win_rows
    )
    dec_valid = jnp.ones(dec_src.shape, jnp.bool_)
    dec_matrix = window_matrix(
        window_slots(dec_src, dec_valid, shard_rows, home_rows, n_mesh, band_index), win_rows
    )
    grid_full = lax.all_gather(grid_in, "feat", axis=1, tiled=True)
    pre_enc = jnp.dot(grid_full, w_enc, preferred_element_type=jnp.float32)
    enc_msg = jax.nn.silu(pre_enc).astype(jnp.bfloat16)
    enc_window = jnp.dot(enc_matrix, enc_msg, preferred_element_type=jnp.float32) * enc_factor
    aggregate_home = band_sum(enc_window, home_rows)
    mesh_home = lax.dynamic_slice_in_dim(mesh_in, home_first, home_rows, 0)
    latent_one = collect_rows((mesh_home.astype(jnp.float32) + aggregate_home).astype(jnp.bfloat16))
    one_full = widen(latent_one)
    pre_proc = jnp.dot(one_full, w_proc, preferred_element_type=jnp.float32)
    proc_msg = jax.nn.silu(pre_proc).astype(jnp.bfloat16)

    def incidence(row_count):
        node_ids = jnp.arange(row_count, dtype=jnp.int32)
        matrix = jnp.zeros((shard_rows, row_count), jnp.bfloat16)
        for column in range(KP):
            matrix = matrix + (proc_src[:, column][:, None] == node_ids[None, :]).astype(
                jnp.bfloat16
            )
        return matrix

    shard_piece = lax.all_gather(proc_msg, "mesh", axis=0, tiled=True)
    neighbour_sum = jnp.dot(
        incidence(shard_piece.shape[0]), shard_piece, preferred_element_type=jnp.float32
    )
    latent_two = (latent_one.astype(jnp.float32) + neighbour_sum / KP).astype(jnp.bfloat16)
    two_full = widen(latent_two)
    pre_dec = jnp.dot(two_full, w_dec, preferred_element_type=jnp.float32)
    dec_window = jnp.dot(dec_matrix, cotangent, preferred_element_type=jnp.float32) / KD
    d_dec = collect_rows(band_sum(dec_window, home_rows).astype(jnp.bfloat16))
    d_pre_dec = (d_dec.astype(jnp.float32) * silu_grad(pre_dec)).astype(jnp.bfloat16)
    d_two = mesh_back(d_pre_dec, w_dec)
    d_two_b = d_two.astype(jnp.bfloat16)
    d_proc = (
        lax.psum_scatter(
            contract_rows(incidence(shard_rows * lax.axis_size("mesh")), d_two_b).astype(
                jnp.bfloat16
            ),
            "mesh",
            scatter_dimension=0,
            tiled=True,
        ).astype(jnp.float32)
        / KP
    )
    d_pre_proc = (d_proc * silu_grad(pre_proc)).astype(jnp.bfloat16)
    d_one = d_two + mesh_back(d_pre_proc, w_proc)
    grad_mesh = d_one.astype(jnp.bfloat16)
    grad_home = lax.dynamic_slice_in_dim(grad_mesh, home_first, home_rows, 0)
    mesh_window = with_halo(grad_home, ((("lat", "mesh"), 0),), home_rows)
    d_enc = contract_rows(enc_matrix, mesh_window) * enc_factor
    d_pre_enc = (d_enc * silu_grad(pre_enc)).astype(jnp.bfloat16)
    grid_terms = lax.psum_scatter(
        back_product(d_pre_enc, w_enc).astype(jnp.bfloat16), "feat", scatter_dimension=1, tiled=True
    ).astype(jnp.float32)
    grad_grid = (cotangent.astype(jnp.float32) + grid_terms).astype(jnp.bfloat16)
    enc_term = contract_rows(grid_full, d_pre_enc)
    grad_w_proc, grad_w_dec = (
        lax.psum(contract_rows(one_full, d_pre_proc).astype(jnp.bfloat16), "mesh").astype(
            jnp.float32
        ),
        lax.psum(contract_rows(two_full, d_pre_dec).astype(jnp.bfloat16), "mesh").astype(
            jnp.float32
        ),
    )
    grad_w_enc = lax.psum(enc_term, ("lat", "mesh"))
    return (grad_grid, grad_mesh, grad_w_enc, grad_w_proc, grad_w_dec)


BF = jnp.bfloat16
F32 = jnp.float32
NN = (((1,), (0,)), ((), ()))
NT = (((1,), (1,)), ((), ()))
TN = (((0,), (0,)), ((), ()))


def mm(left, right, dims=NN):
    return lax.dot_general(left, right, dims, preferred_element_type=F32)


def sigm(value):
    return 1.0 / (1.0 + jnp.exp(-value))


def fused_kernel(
    n_lat, n_mesh,
    grid_ref, mesh_ref, we_ref, wp_ref, wd_ref, gi_ref, pi_ref, cot_ref,
    gg_ref, gm_ref, gwe_ref, gwp_ref, gwd_ref,
    gfull, wef, wpf, wdf, psall, pst, idt, enc_m, enc_t, dec_m, inc_a, inc_t,
    halo_out, halo_in, own_win, sg_enc, one, ddec, sg_proc, pmsg, two, dpd, dtwo, dtwo_b, dpp,
    gmesh, dpe, dwin, rs_src, rs_own, rs_in, ag,
    s_f, r_f, s_p, r_p, s_h, r_h, s_z, r_z, s_x, r_x, s_c, r_c, s_rs, r_rs, s_ag, r_ag,
):
    rows, half = grid_ref.shape
    shard = mesh_ref.shape[0]
    home = shard // n_lat
    bands = n_lat * n_mesh
    nodes = shard * n_mesh
    wide = 2 * half
    chunk = wide // bands
    win = 3 * home
    factor = home / rows
    l = lax.axis_index("lat")
    m = lax.axis_index("mesh")
    f = lax.axis_index("feat")
    b = l * n_mesh + m
    mine = pl.ds(pl.multiple_of(f * half, half), half)

    def remote(source, target, send, recv, **where):
        return pltpu.make_async_remote_copy(
            src_ref=source, dst_ref=target, send_sem=send, recv_sem=recv,
            device_id=where, device_id_type=pl.DeviceIdType.MESH,
        )

    def band_at(index):
        return {"lat": index // n_mesh, "mesh": lax.rem(index, n_mesh)}

    barrier = pltpu.get_barrier_semaphore()
    for d in range(1, bands):
        pl.semaphore_signal(
            barrier, inc=1, device_id=band_at(lax.rem(b + d, bands)),
            device_id_type=pl.DeviceIdType.MESH,
        )
    pl.semaphore_signal(
        barrier, inc=1, device_id={"feat": 1 - f}, device_id_type=pl.DeviceIdType.MESH
    )

    raw = gi_ref[...]
    inner = raw & (shard - 1)
    home_id = (inner >> (home.bit_length() - 1)) * n_mesh + (raw >> (shard.bit_length() - 1))
    ids = (home_id - b + 1) * home + (inner & (home - 1))
    row = lax.broadcasted_iota(jnp.int32, raw.shape, 0)
    ids = jnp.where((row < KE) & (row >= raw[KE:KE + 1, :]), -1, ids)
    idt[...] = ids.astype(F32).T

    def one_hot(target, first, count):
        step = 64
        for r in range(0, win, step):
            node = lax.broadcasted_iota(jnp.int32, (step, rows), 0) + r
            acc = jnp.zeros((step, rows), F32)
            for k in range(first, first + count):
                acc = acc + jnp.where(node == ids[k:k + 1, :], 1.0, 0.0)
            target[r:r + step, :] = acc.astype(BF)

    one_hot(dec_m, KE + 1, KD)
    dec_win = mm(dec_m[...], cot_ref[...]) / KD
    halo_out[0] = dec_win[2 * home:, :].astype(BF)
    halo_out[1] = dec_win[:home, :].astype(BF)
    own_win[0] = dec_win[home:2 * home, :]
    one_hot(enc_m, 0, KE)
    gfull[:, mine] = grid_ref[...]
    wef[:, mine] = we_ref[...]
    wpf[:, mine] = wp_ref[...]
    wdf[:, mine] = wd_ref[...]
    psall[m] = pi_ref[...]

    @pl.when(b == 0)
    def _():
        halo_in[0] = jnp.zeros((home, half), BF)
        halo_in[2] = jnp.zeros((home, half), BF)

    @pl.when(b == bands - 1)
    def _():
        halo_in[1] = jnp.zeros((home, half), BF)
        halo_in[3] = jnp.zeros((home, half), BF)

    pl.semaphore_wait(barrier, bands)

    wides = [
        remote(s, t.at[:, mine], s_f.at[i], r_f.at[i], feat=1 - f)
        for i, (s, t) in enumerate(
            ((grid_ref, gfull), (we_ref, wef), (wp_ref, wpf), (wd_ref, wdf))
        )
    ]
    indices = [
        remote(pi_ref, psall.at[m], s_p.at[e - 1], r_p.at[e - 1], mesh=lax.rem(m + e, n_mesh))
        for e in range(1, n_mesh)
    ]
    wides[0].start()

    def halo(i, up):
        slot = 2 * i + (0 if up else 1)
        return remote(
            halo_out.at[slot], halo_in.at[slot], s_h.at[slot], r_h.at[slot],
            **band_at(b + 1 if up else b - 1),
        )

    def halo_start(i):
        @pl.when(b < bands - 1)
        def _():
            halo(i, True).start()

        @pl.when(b > 0)
        def _():
            halo(i, False).start()

    def halo_recv(i):
        @pl.when(b > 0)
        def _():
            halo(i, True).wait_recv()

        @pl.when(b < bands - 1)
        def _():
            halo(i, False).wait_recv()

    def halo_sent(i):
        @pl.when(b < bands - 1)
        def _():
            halo(i, True).wait_send()

        @pl.when(b > 0)
        def _():
            halo(i, False).wait_send()

    halo_start(0)
    for copy in indices + wides[1:]:
        copy.start()

    wides[0].wait_recv()
    pre = mm(gfull[...], we_ref[...])
    enc_win = mm(enc_m[...], (pre * sigm(pre)).astype(BF)) * factor
    halo_out[2] = enc_win[2 * home:, :].astype(BF)
    halo_out[3] = enc_win[:home, :].astype(BF)
    own_win[1] = enc_win[home:2 * home, :]
    halo_start(1)

    for copy in indices:
        copy.wait_recv()
    step = 64
    for i in range(n_mesh):
        pst[i * shard:(i + 1) * shard, :] = psall[i].astype(F32).T

    def build_a(t, carry):
        r = pl.multiple_of(t * step, step)
        node = lax.broadcasted_iota(jnp.int32, (step, nodes), 1).astype(F32)
        acc = jnp.zeros((step, nodes), F32)
        for k in range(KP):
            acc = acc + jnp.where(node == pst[pl.ds(r, step), k:k + 1], 1.0, 0.0)
        inc_a[pl.ds(r, step), :] = acc.astype(BF)
        return carry

    def build_t(t, carry):
        r = pl.multiple_of(t * step, step)
        for i in range(n_mesh):
            node = lax.broadcasted_iota(jnp.int32, (step, shard), 0) + r
            acc = jnp.zeros((step, shard), F32)
            for k in range(KP):
                acc = acc + jnp.where(node == psall[i, k:k + 1, :], 1.0, 0.0)
            inc_t[pl.ds(r, step), i * shard:(i + 1) * shard] = acc.astype(BF)
        return carry

    def build_e(t, carry):
        r = pl.multiple_of(t * step, step)
        node = lax.broadcasted_iota(jnp.int32, (step, win), 1).astype(F32)
        acc = jnp.zeros((step, win), F32)
        for k in range(KE):
            acc = acc + jnp.where(node == idt[pl.ds(r, step), k:k + 1], 1.0, 0.0)
        enc_t[pl.ds(r, step), :] = acc.astype(BF)
        return carry

    def block(array, d, e):
        at_l = lax.rem(l + n_lat - d, n_lat)
        at_m = lax.rem(m + n_mesh - e, n_mesh)
        return array.at[pl.ds(pl.multiple_of(at_m * shard + at_l * home, home), home), mine]

    def along_lat(array, a, d):
        own = block(array, 0, 0)
        return remote(own, own, s_z.at[a, d - 1], r_z.at[a, d - 1], lat=lax.rem(l + d, n_lat))

    def recv_lat(array, a, d):
        view = block(array, d, 0)
        return remote(view, view, s_z.at[a, d - 1], r_z.at[a, d - 1], lat=lax.rem(l + d, n_lat))

    def along_mesh(array, a, d, e):
        view = block(array, d, 0)
        return remote(
            view, view, s_x.at[a, d, e - 1], r_x.at[a, d, e - 1], mesh=lax.rem(m + e, n_mesh)
        )

    def recv_mesh(array, a, d, e):
        view = block(array, d, e)
        return remote(
            view, view, s_x.at[a, d, e - 1], r_x.at[a, d, e - 1], mesh=lax.rem(m + e, n_mesh)
        )

    def along_feat(array, a, d, e):
        view = block(array, d, e)
        return remote(view, view, s_c.at[a, d, e], r_c.at[a, d, e], feat=1 - f)

    def spread_own(array, a):
        for e in range(1, n_mesh):
            along_mesh(array, a, 0, e).start()
        for d in range(1, n_lat):
            along_lat(array, a, d).start()
        along_feat(array, a, 0, 0).start()

    def spread_lat(array, a):
        for d in range(1, n_lat):
            recv_lat(array, a, d).wait_recv()
            for e in range(1, n_mesh):
                along_mesh(array, a, d, e).start()
            along_feat(array, a, d, 0).start()

    def spread_mesh(array, a):
        for d in range(n_lat):
            for e in range(1, n_mesh):
                recv_mesh(array, a, d, e).wait_recv()
                along_feat(array, a, d, e).start()

    def spread_done(array, a):
        for d in range(n_lat):
            for e in range(n_mesh):
                along_feat(array, a, d, e).wait_recv()

    def spread_sent(array, a):
        for d in range(1, n_lat):
            along_lat(array, a, d).wait_send()
        for d in range(n_lat):
            for e in range(n_mesh):
                if e:
                    along_mesh(array, a, d, e).wait_send()
                along_feat(array, a, d, e).wait_send()

    def banded(i):
        return own_win[i] + halo_in[2 * i].astype(F32) + halo_in[2 * i + 1].astype(F32)

    home_rows = pl.ds(pl.multiple_of(m * shard + l * home, home), home)
    halo_recv(0)
    ddec[home_rows, mine] = banded(0).astype(BF)
    halo_recv(1)
    mesh_home = mesh_ref[pl.ds(pl.multiple_of(l * home, home), home), :].astype(F32)
    one[home_rows, mine] = (mesh_home + banded(1)).astype(BF)
    spread_own(one, 0)
    lax.fori_loop(0, nodes // step, build_a, 0)
    spread_lat(one, 0)
    spread_own(ddec, 1)
    spread_mesh(one, 0)
    lax.fori_loop(0, nodes // step, build_t, 0)
    spread_lat(ddec, 1)
    wides[1].wait_recv()
    wides[2].wait_recv()
    wides[3].wait_recv()
    tile = min(512, nodes)
    spread_done(one, 0)

    def tiles(body):
        for r in range(0, nodes, tile):
            body(slice(r, r + tile))

    def proc(at):
        value = mm(one[at, :], wpf[...])
        sig = sigm(value)
        pmsg[at, :] = (value * sig).astype(BF)
        sg_proc[at, :] = sig * (1.0 + value * (1.0 - sig))

    tiles(proc)
    spread_mesh(ddec, 1)

    def second(at):
        total = mm(inc_a[at, :], pmsg[...])
        two[at, :] = (one[at, :].astype(F32) + total * (1.0 / KP)).astype(BF)

    tiles(second)

    pre_all = mm(gfull[...], wef[...])
    sig_all = sigm(pre_all)
    sg_enc[...] = sig_all * (1.0 + pre_all * (1.0 - sig_all))
    lax.fori_loop(0, rows // step, build_e, 0)
    spread_done(ddec, 1)

    def decode(at):
        value = mm(two[at, :], wdf[...])
        sig = sigm(value)
        grad = sig * (1.0 + value * (1.0 - sig))
        dpd[at, :] = (ddec[at, :].astype(F32) * grad).astype(BF)
        back = mm(dpd[at, :], wdf[...], NT)
        dtwo[at, :] = back
        dtwo_b[at, :] = back.astype(BF)

    tiles(decode)

    def third(at):
        total = mm(inc_t[at, :], dtwo_b[...]) * (1.0 / KP)
        dpp[at, :] = (total * sg_proc[at, :]).astype(BF)
        gmesh[at, :] = (dtwo[at, :] + mm(dpp[at, :], wpf[...], NT)).astype(BF)

    tiles(third)

    for j in range(3):
        at = jnp.clip(b + j - 1, 0, bands - 1)
        first = pl.multiple_of(lax.rem(at, n_mesh) * shard + at // n_mesh * home, home)
        dwin[j * home:(j + 1) * home, :] = gmesh[pl.ds(first, home), :]
    dpe[...] = (mm(enc_t[...], dwin[...]) * factor * sg_enc[...]).astype(BF)
    weight = mm(gfull[...], dpe[:, mine], TN)
    rs_own[...] = weight
    rs_src[...] = weight.astype(BF)

    def part(index):
        return pl.ds(pl.multiple_of(index * chunk, chunk), chunk)

    scatter, gather = [], []
    for d in range(1, bands):
        to = lax.rem(b + d, bands)
        scatter.append(
            remote(
                rs_src.at[part(to), :], rs_in.at[d - 1], s_rs.at[d - 1], r_rs.at[d - 1],
                **band_at(to),
            )
        )
        scatter[-1].start()
    gwd_ref[...] = mm(two[...], dpd[:, mine], TN)
    gwp_ref[...] = mm(one[...], dpp[:, mine], TN)
    total = rs_own[part(b), :]
    for d in range(1, bands):
        scatter[d - 1].wait_recv()
        total = total + rs_in[d - 1].astype(F32)
    ag[part(b), :] = total.astype(BF)
    for d in range(1, bands):
        gather.append(
            remote(
                ag.at[part(b), :], ag.at[part(b), :], s_ag.at[d - 1], r_ag.at[d - 1],
                **band_at(lax.rem(b + d, bands)),
            )
        )
        gather[-1].start()
    terms = mm(dpe[...], wef[mine, :], NT)
    gg_ref[...] = (cot_ref[...].astype(F32) + terms).astype(BF)
    gm_ref[...] = gmesh[pl.ds(pl.multiple_of(m * shard, shard), shard), mine]
    for copy in wides + indices:
        copy.wait_send()
    halo_sent(0)
    halo_sent(1)
    spread_sent(one, 0)
    spread_sent(ddec, 1)
    for copy in scatter:
        copy.wait_send()
    for d in range(1, bands):
        view = ag.at[part(lax.rem(b + bands - d, bands)), :]
        remote(
            view, view, s_ag.at[d - 1], r_ag.at[d - 1], **band_at(lax.rem(b + d, bands))
        ).wait_recv()
    gwe_ref[...] = ag[...].astype(F32)
    for copy in gather:
        copy.wait_send()


def local_fused(
    grid_in, mesh_in, w_enc, w_proc, w_dec, enc_dst, enc_count, dec_src, proc_src, cotangent
):
    n_mesh = lax.axis_size("mesh")
    n_lat = lax.axis_size("lat")
    rows, half = grid_in.shape
    shard = mesh_in.shape[0]
    wide = 2 * half
    home = shard // n_lat
    bands = n_lat * n_mesh
    nodes = shard * n_mesh
    win = 3 * home
    grid_index = jnp.concatenate([enc_dst.T, enc_count[None, :], dec_src.T], axis=0)
    node_index = jnp.pad(proc_src.T, ((0, 8 - KP), (0, 0)))
    v = pltpu.VMEM
    dma = pltpu.SemaphoreType.DMA
    vmem = pl.BlockSpec(memory_space=pltpu.VMEM)
    shaped = jax.ShapeDtypeStruct
    return tuple(pl.pallas_call(
        functools.partial(fused_kernel, n_lat, n_mesh),
        out_shape=(
            shaped((rows, half), BF),
            shaped((shard, half), BF),
            shaped((wide, half), F32),
            shaped((wide, half), F32),
            shaped((wide, half), F32),
        ),
        in_specs=[vmem] * 8,
        out_specs=(vmem,) * 5,
        scratch_shapes=[
            v((rows, wide), BF), v((wide, wide), BF), v((wide, wide), BF), v((wide, wide), BF),
            v((n_mesh, 8, shard), jnp.int32), v((nodes, 8), F32), v((rows, 8), F32),
            v((win, rows), BF), v((rows, win), BF), v((win, rows), BF),
            v((nodes, nodes), BF), v((nodes, nodes), BF),
            v((4, home, half), BF), v((4, home, half), BF), v((2, home, half), F32),
            v((rows, wide), F32),
            v((nodes, wide), BF), v((nodes, wide), BF), v((nodes, wide), F32),
            v((nodes, wide), BF), v((nodes, wide), BF), v((nodes, wide), BF),
            v((nodes, wide), F32), v((nodes, wide), BF), v((nodes, wide), BF),
            v((nodes, wide), BF), v((rows, wide), BF), v((win, wide), BF),
            v((wide, half), BF), v((wide, half), F32),
            v((bands - 1, wide // bands, half), BF), v((wide, half), BF),
            dma((4,)), dma((4,)), dma((n_mesh - 1,)), dma((n_mesh - 1,)),
            dma((4,)), dma((4,)),
            dma((2, n_lat - 1)), dma((2, n_lat - 1)),
            dma((2, n_lat, n_mesh - 1)), dma((2, n_lat, n_mesh - 1)),
            dma((2, n_lat, n_mesh)), dma((2, n_lat, n_mesh)),
            dma((bands - 1,)), dma((bands - 1,)), dma((bands - 1,)), dma((bands - 1,)),
        ],
        compiler_params=pltpu.CompilerParams(
            collective_id=0, has_side_effects=True, vmem_limit_bytes=56 * 1024 * 1024
        ),
        cost_estimate=pl.CostEstimate(
            flops=10 * nodes * wide * wide, bytes_accessed=8 * rows * wide,
            transcendentals=4 * nodes * wide,
        ),
    )(grid_in, mesh_in, w_enc, w_proc, w_dec, grid_index, node_index, cotangent))


def solution(mesh):
    bands = mesh.shape["lat"] * mesh.shape["mesh"]
    body = local_fused if bands <= 8 and mesh.shape["feat"] == 2 else local_staged
    placed = (
        P(("groups", "lat", "mesh"), "feat"),
        P(("groups", "mesh"), "feat"),
        P(None, "feat"),
        P(None, "feat"),
        P(None, "feat"),
        P(("groups", "lat", "mesh"), None),
        P(("groups", "lat", "mesh")),
        P(("groups", "lat", "mesh"), None),
        P(("groups", "mesh"), None),
        P(("groups", "lat", "mesh"), "feat"),
    )
    return jax.shard_map(
        body,
        mesh=mesh,
        in_specs=placed,
        out_specs=(
            P(("groups", "lat", "mesh"), "feat"),
            P(("groups", "mesh"), "feat"),
            P("groups", "feat"),
            P("groups", "feat"),
            P("groups", "feat"),
        ),
        check_vma=False,
    )
```

```python
import functools

import jax
import jax.numpy as jnp
from jax import lax
from jax.experimental import pallas as pl
from jax.experimental.pallas import tpu as pltpu
from jax.sharding import PartitionSpec as P

KE = 4
KD = 3
KP = 6


def with_halo(value, sides, width):
    for axis, dim in sides:
        size, length = (lax.axis_size(axis), value.shape[dim])
        up = [(i, (i + 1) % size) for i in range(size - 1)]
        down = [(j, i) for i, j in up]
        last = lax.slice_in_dim(value, length - width, length, axis=dim)
        first = lax.slice_in_dim(value, 0, width, axis=dim)
        before = lax.ppermute(last, axis, up)
        after = lax.ppermute(first, axis, down)
        value = jnp.concatenate([before, value, after], axis=dim)
    return value


def silu_grad(pre):
    sig = jax.nn.sigmoid(pre)
    return sig * (1.0 + pre * (1.0 - sig))


def window_slots(targets, is_valid, shard_rows, home_rows, n_mesh, band_index):
    owner_shard = targets // shard_rows
    inner_row = targets % shard_rows
    home_id = inner_row // home_rows * n_mesh + owner_shard
    slot_ids = (home_id - band_index + 1) * home_rows + inner_row % home_rows
    return jnp.where(is_valid, slot_ids, -1)


def window_matrix(slot_ids, win_rows):
    row_ids = jnp.arange(win_rows, dtype=jnp.int32)[:, None]
    matrix = jnp.zeros((win_rows, slot_ids.shape[0]), jnp.bfloat16)
    for column in range(slot_ids.shape[1]):
        matrix = matrix + (row_ids == slot_ids[:, column][None, :]).astype(jnp.bfloat16)
    return matrix


def band_sum(window, home_rows):
    stacked = window.reshape(3, home_rows, window.shape[1])
    padded_win = with_halo(stacked.astype(jnp.bfloat16), ((("lat", "mesh"), 0),), 3).astype(
        stacked.dtype
    )
    return padded_win[2] + padded_win[4] + padded_win[6]


def collect_rows(home_block):
    return lax.all_gather(home_block, "lat", axis=0, tiled=True)


def widen(latent):
    return lax.all_gather(latent, "feat", axis=1, tiled=True)


def back_product(d_pre, weight):
    return lax.dot_general(
        d_pre, weight, (((1,), (1,)), ((), ())), preferred_element_type=jnp.float32
    )


def mesh_back(d_pre, weight):
    return lax.psum_scatter(
        back_product(d_pre, weight).astype(jnp.bfloat16), "feat", scatter_dimension=1, tiled=True
    ).astype(jnp.float32)


def contract_rows(left_rows, right_rows):
    return lax.dot_general(
        left_rows, right_rows, (((0,), (0,)), ((), ())), preferred_element_type=jnp.float32
    )


def local_staged(grid_in, mesh_in, w_enc, w_proc, w_dec, enc_dst, enc_count, dec_src, proc_src, cotangent):
    n_mesh = lax.axis_size("mesh")
    n_lat = lax.axis_size("lat")
    shard_rows = mesh_in.shape[0]
    home_rows = shard_rows // n_lat
    grid_rows = grid_in.shape[0]
    enc_factor = home_rows / grid_rows
    band_index = lax.axis_index("lat") * n_mesh + lax.axis_index("mesh")
    home_first = lax.axis_index("lat") * home_rows
    win_rows = 3 * home_rows
    enc_valid = jnp.arange(KE, dtype=jnp.int32)[None, :] < enc_count[:, None]
    enc_matrix = window_matrix(
        window_slots(enc_dst, enc_valid, shard_rows, home_rows, n_mesh, band_index), win_rows
    )
    dec_valid = jnp.ones(dec_src.shape, jnp.bool_)
    dec_matrix = window_matrix(
        window_slots(dec_src, dec_valid, shard_rows, home_rows, n_mesh, band_index), win_rows
    )
    grid_full = lax.all_gather(grid_in, "feat", axis=1, tiled=True)
    pre_enc = jnp.dot(grid_full, w_enc, preferred_element_type=jnp.float32)
    enc_msg = jax.nn.silu(pre_enc).astype(jnp.bfloat16)
    enc_window = jnp.dot(enc_matrix, enc_msg, preferred_element_type=jnp.float32) * enc_factor
    aggregate_home = band_sum(enc_window, home_rows)
    mesh_home = lax.dynamic_slice_in_dim(mesh_in, home_first, home_rows, 0)
    latent_one = collect_rows((mesh_home.astype(jnp.float32) + aggregate_home).astype(jnp.bfloat16))
    one_full = widen(latent_one)
    pre_proc = jnp.dot(one_full, w_proc, preferred_element_type=jnp.float32)
    proc_msg = jax.nn.silu(pre_proc).astype(jnp.bfloat16)

    def incidence(row_count):
        node_ids = jnp.arange(row_count, dtype=jnp.int32)
        matrix = jnp.zeros((shard_rows, row_count), jnp.bfloat16)
        for column in range(KP):
            matrix = matrix + (proc_src[:, column][:, None] == node_ids[None, :]).astype(
                jnp.bfloat16
            )
        return matrix

    shard_piece = lax.all_gather(proc_msg, "mesh", axis=0, tiled=True)
    neighbour_sum = jnp.dot(
        incidence(shard_piece.shape[0]), shard_piece, preferred_element_type=jnp.float32
    )
    latent_two = (latent_one.astype(jnp.float32) + neighbour_sum / KP).astype(jnp.bfloat16)
    two_full = widen(latent_two)
    pre_dec = jnp.dot(two_full, w_dec, preferred_element_type=jnp.float32)
    dec_window = jnp.dot(dec_matrix, cotangent, preferred_element_type=jnp.float32) / KD
    d_dec = collect_rows(band_sum(dec_window, home_rows).astype(jnp.bfloat16))
    d_pre_dec = (d_dec.astype(jnp.float32) * silu_grad(pre_dec)).astype(jnp.bfloat16)
    d_two = mesh_back(d_pre_dec, w_dec)
    d_two_b = d_two.astype(jnp.bfloat16)
    d_proc = (
        lax.psum_scatter(
            contract_rows(incidence(shard_rows * lax.axis_size("mesh")), d_two_b).astype(
                jnp.bfloat16
            ),
            "mesh",
            scatter_dimension=0,
            tiled=True,
        ).astype(jnp.float32)
        / KP
    )
    d_pre_proc = (d_proc * silu_grad(pre_proc)).astype(jnp.bfloat16)
    d_one = d_two + mesh_back(d_pre_proc, w_proc)
    grad_mesh = d_one.astype(jnp.bfloat16)
    grad_home = lax.dynamic_slice_in_dim(grad_mesh, home_first, home_rows, 0)
    mesh_window = with_halo(grad_home, ((("lat", "mesh"), 0),), home_rows)
    d_enc = contract_rows(enc_matrix, mesh_window) * enc_factor
    d_pre_enc = (d_enc * silu_grad(pre_enc)).astype(jnp.bfloat16)
    grid_terms = lax.psum_scatter(
        back_product(d_pre_enc, w_enc).astype(jnp.bfloat16), "feat", scatter_dimension=1, tiled=True
    ).astype(jnp.float32)
    grad_grid = (cotangent.astype(jnp.float32) + grid_terms).astype(jnp.bfloat16)
    enc_term = contract_rows(grid_full, d_pre_enc)
    grad_w_proc, grad_w_dec = (
        lax.psum(contract_rows(one_full, d_pre_proc).astype(jnp.bfloat16), "mesh").astype(
            jnp.float32
        ),
        lax.psum(contract_rows(two_full, d_pre_dec).astype(jnp.bfloat16), "mesh").astype(
            jnp.float32
        ),
    )
    grad_w_enc = lax.psum(enc_term, ("lat", "mesh"))
    return (grad_grid, grad_mesh, grad_w_enc, grad_w_proc, grad_w_dec)


BF = jnp.bfloat16
F32 = jnp.float32
NN = (((1,), (0,)), ((), ()))
NT = (((1,), (1,)), ((), ()))
TN = (((0,), (0,)), ((), ()))


def mm(left, right, dims=NN):
    return lax.dot_general(left, right, dims, preferred_element_type=F32)


def sigm(value):
    return 1.0 / (1.0 + jnp.exp(-value))


def fused_kernel(
    n_lat, n_mesh,
    grid_ref, mesh_ref, we_ref, wp_ref, wd_ref, dst_ref, count_ref, src_ref, pi_ref, cot_ref,
    gg_ref, gm_ref, gwe_ref, gwp_ref, gwd_ref,
    gfull, wef, wpf, wdf, stage, psall, pst, idt, enc_m, enc_t, dec_m, inc_a, inc_t,
    halo_out, halo_in, own_win, sg_enc, one, ddec, sg_proc, pmsg, two, dpd, dtwo, dtwo_b, dpp,
    gmesh, dpe, dwin, rs_src, rs_own, rs_in, ag,
    s_f, r_f, s_p, r_p, s_h, r_h, s_z, r_z, s_x, r_x, s_c, r_c, s_rs, r_rs, s_ag, r_ag,
):
    rows, half = grid_ref.shape
    shard = mesh_ref.shape[0]
    home = shard // n_lat
    bands = n_lat * n_mesh
    nodes = shard * n_mesh
    wide = 2 * half
    chunk = wide // bands
    win = 3 * home
    factor = home / rows
    l = lax.axis_index("lat")
    m = lax.axis_index("mesh")
    f = lax.axis_index("feat")
    b = l * n_mesh + m
    mine = pl.ds(pl.multiple_of(f * half, half), half)

    def remote(source, target, send, recv, **where):
        return pltpu.make_async_remote_copy(
            src_ref=source, dst_ref=target, send_sem=send, recv_sem=recv,
            device_id=where, device_id_type=pl.DeviceIdType.MESH,
        )

    def band_at(index):
        return {"lat": index // n_mesh, "mesh": lax.rem(index, n_mesh)}

    barrier = pltpu.get_barrier_semaphore()
    for d in range(1, bands):
        pl.semaphore_signal(
            barrier, inc=1, device_id=band_at(lax.rem(b + d, bands)),
            device_id_type=pl.DeviceIdType.MESH,
        )
    pl.semaphore_signal(
        barrier, inc=1, device_id={"feat": 1 - f}, device_id_type=pl.DeviceIdType.MESH
    )

    def slots(raw):
        inner = raw & (shard - 1)
        home_id = (inner >> (home.bit_length() - 1)) * n_mesh + (raw >> (shard.bit_length() - 1))
        return (home_id - b + 1) * home + (inner & (home - 1))

    order = lax.broadcasted_iota(jnp.int32, dst_ref.shape, 0)
    enc_ids = jnp.where(order < count_ref[...], slots(dst_ref[...]), -1)
    dec_ids = slots(src_ref[...])
    idt[...] = jnp.concatenate([enc_ids, enc_ids], axis=0).astype(F32).T
    stage[0:KP, :] = pi_ref[...]
    stage[KP:8, :] = jnp.zeros((8 - KP, shard), jnp.int32)

    def one_hot(target, ids):
        step = 64
        for r in range(0, win, step):
            node = lax.broadcasted_iota(jnp.int32, (step, rows), 0) + r
            acc = jnp.zeros((step, rows), F32)
            for k in range(ids.shape[0]):
                acc = acc + jnp.where(node == ids[k:k + 1, :], 1.0, 0.0)
            target[r:r + step, :] = acc.astype(BF)

    one_hot(dec_m, dec_ids)
    dec_win = mm(dec_m[...], cot_ref[...]) / KD
    halo_out[0] = dec_win[2 * home:, :].astype(BF)
    halo_out[1] = dec_win[:home, :].astype(BF)
    own_win[0] = dec_win[home:2 * home, :]
    one_hot(enc_m, enc_ids)
    gfull[:, mine] = grid_ref[...]
    wef[:, mine] = we_ref[...]
    wpf[:, mine] = wp_ref[...]
    wdf[:, mine] = wd_ref[...]
    psall[m] = stage[...]

    @pl.when(b == 0)
    def _():
        halo_in[0] = jnp.zeros((home, half), BF)
        halo_in[2] = jnp.zeros((home, half), BF)

    @pl.when(b == bands - 1)
    def _():
        halo_in[1] = jnp.zeros((home, half), BF)
        halo_in[3] = jnp.zeros((home, half), BF)

    pl.semaphore_wait(barrier, bands)

    wides = [
        remote(s, t.at[:, mine], s_f.at[i], r_f.at[i], feat=1 - f)
        for i, (s, t) in enumerate(
            ((grid_ref, gfull), (we_ref, wef), (wp_ref, wpf), (wd_ref, wdf))
        )
    ]
    indices = [
        remote(stage, psall.at[m], s_p.at[e - 1], r_p.at[e - 1], mesh=lax.rem(m + e, n_mesh))
        for e in range(1, n_mesh)
    ]
    wides[0].start()

    def halo(i, up):
        slot = 2 * i + (0 if up else 1)
        return remote(
            halo_out.at[slot], halo_in.at[slot], s_h.at[slot], r_h.at[slot],
            **band_at(b + 1 if up else b - 1),
        )

    def halo_start(i):
        @pl.when(b < bands - 1)
        def _():
            halo(i, True).start()

        @pl.when(b > 0)
        def _():
            halo(i, False).start()

    def halo_recv(i):
        @pl.when(b > 0)
        def _():
            halo(i, True).wait_recv()

        @pl.when(b < bands - 1)
        def _():
            halo(i, False).wait_recv()

    def halo_sent(i):
        @pl.when(b < bands - 1)
        def _():
            halo(i, True).wait_send()

        @pl.when(b > 0)
        def _():
            halo(i, False).wait_send()

    halo_start(0)
    for copy in indices + wides[1:]:
        copy.start()

    wides[0].wait_recv()
    pre = mm(gfull[...], we_ref[...])
    enc_win = mm(enc_m[...], (pre * sigm(pre)).astype(BF)) * factor
    halo_out[2] = enc_win[2 * home:, :].astype(BF)
    halo_out[3] = enc_win[:home, :].astype(BF)
    own_win[1] = enc_win[home:2 * home, :]
    halo_start(1)

    for copy in indices:
        copy.wait_recv()
    step = 64
    for i in range(n_mesh):
        pst[i * shard:(i + 1) * shard, :] = psall[i].astype(F32).T

    def build_a(t, carry):
        r = pl.multiple_of(t * step, step)
        node = lax.broadcasted_iota(jnp.int32, (step, nodes), 1).astype(F32)
        acc = jnp.zeros((step, nodes), F32)
        for k in range(KP):
            acc = acc + jnp.where(node == pst[pl.ds(r, step), k:k + 1], 1.0, 0.0)
        inc_a[pl.ds(r, step), :] = acc.astype(BF)
        return carry

    def build_t(t, carry):
        r = pl.multiple_of(t * step, step)
        for i in range(n_mesh):
            node = lax.broadcasted_iota(jnp.int32, (step, shard), 0) + r
            acc = jnp.zeros((step, shard), F32)
            for k in range(KP):
                acc = acc + jnp.where(node == psall[i, k:k + 1, :], 1.0, 0.0)
            inc_t[pl.ds(r, step), i * shard:(i + 1) * shard] = acc.astype(BF)
        return carry

    def build_e(t, carry):
        r = pl.multiple_of(t * step, step)
        node = lax.broadcasted_iota(jnp.int32, (step, win), 1).astype(F32)
        acc = jnp.zeros((step, win), F32)
        for k in range(KE):
            acc = acc + jnp.where(node == idt[pl.ds(r, step), k:k + 1], 1.0, 0.0)
        enc_t[pl.ds(r, step), :] = acc.astype(BF)
        return carry

    def block(array, d, e):
        at_l = lax.rem(l + n_lat - d, n_lat)
        at_m = lax.rem(m + n_mesh - e, n_mesh)
        return array.at[pl.ds(pl.multiple_of(at_m * shard + at_l * home, home), home), mine]

    def along_lat(array, a, d):
        own = block(array, 0, 0)
        return remote(own, own, s_z.at[a, d - 1], r_z.at[a, d - 1], lat=lax.rem(l + d, n_lat))

    def recv_lat(array, a, d):
        view = block(array, d, 0)
        return remote(view, view, s_z.at[a, d - 1], r_z.at[a, d - 1], lat=lax.rem(l + d, n_lat))

    def along_mesh(array, a, d, e):
        view = block(array, d, 0)
        return remote(
            view, view, s_x.at[a, d, e - 1], r_x.at[a, d, e - 1], mesh=lax.rem(m + e, n_mesh)
        )

    def recv_mesh(array, a, d, e):
        view = block(array, d, e)
        return remote(
            view, view, s_x.at[a, d, e - 1], r_x.at[a, d, e - 1], mesh=lax.rem(m + e, n_mesh)
        )

    def along_feat(array, a, d, e):
        view = block(array, d, e)
        return remote(view, view, s_c.at[a, d, e], r_c.at[a, d, e], feat=1 - f)

    def spread_own(array, a):
        for e in range(1, n_mesh):
            along_mesh(array, a, 0, e).start()
        for d in range(1, n_lat):
            along_lat(array, a, d).start()
        along_feat(array, a, 0, 0).start()

    def spread_lat(array, a):
        for d in range(1, n_lat):
            recv_lat(array, a, d).wait_recv()
            for e in range(1, n_mesh):
                along_mesh(array, a, d, e).start()
            along_feat(array, a, d, 0).start()

    def spread_mesh(array, a):
        for d in range(n_lat):
            for e in range(1, n_mesh):
                recv_mesh(array, a, d, e).wait_recv()
                along_feat(array, a, d, e).start()

    def spread_done(array, a):
        for d in range(n_lat):
            for e in range(n_mesh):
                along_feat(array, a, d, e).wait_recv()

    def spread_sent(array, a):
        for d in range(1, n_lat):
            along_lat(array, a, d).wait_send()
        for d in range(n_lat):
            for e in range(n_mesh):
                if e:
                    along_mesh(array, a, d, e).wait_send()
                along_feat(array, a, d, e).wait_send()

    def banded(i):
        return own_win[i] + halo_in[2 * i].astype(F32) + halo_in[2 * i + 1].astype(F32)

    home_rows = pl.ds(pl.multiple_of(m * shard + l * home, home), home)
    halo_recv(0)
    ddec[home_rows, mine] = banded(0).astype(BF)
    halo_recv(1)
    mesh_home = mesh_ref[pl.ds(pl.multiple_of(l * home, home), home), :].astype(F32)
    one[home_rows, mine] = (mesh_home + banded(1)).astype(BF)
    spread_own(one, 0)
    lax.fori_loop(0, nodes // step, build_a, 0)
    spread_lat(one, 0)
    spread_own(ddec, 1)
    spread_mesh(one, 0)
    lax.fori_loop(0, nodes // step, build_t, 0)
    spread_lat(ddec, 1)
    wides[1].wait_recv()
    wides[2].wait_recv()
    wides[3].wait_recv()
    tile = min(512, nodes)
    spread_done(one, 0)

    def tiles(body):
        for r in range(0, nodes, tile):
            body(slice(r, r + tile))

    def proc(at):
        value = mm(one[at, :], wpf[...])
        sig = sigm(value)
        pmsg[at, :] = (value * sig).astype(BF)
        sg_proc[at, :] = sig * (1.0 + value * (1.0 - sig))

    tiles(proc)
    spread_mesh(ddec, 1)

    def second(at):
        total = mm(inc_a[at, :], pmsg[...])
        two[at, :] = (one[at, :].astype(F32) + total * (1.0 / KP)).astype(BF)

    tiles(second)

    pre_all = mm(gfull[...], wef[...])
    sig_all = sigm(pre_all)
    sg_enc[...] = sig_all * (1.0 + pre_all * (1.0 - sig_all))
    lax.fori_loop(0, rows // step, build_e, 0)
    spread_done(ddec, 1)

    def decode(at):
        value = mm(two[at, :], wdf[...])
        sig = sigm(value)
        grad = sig * (1.0 + value * (1.0 - sig))
        dpd[at, :] = (ddec[at, :].astype(F32) * grad).astype(BF)
        back = mm(dpd[at, :], wdf[...], NT)
        dtwo[at, :] = back
        dtwo_b[at, :] = back.astype(BF)

    tiles(decode)

    def third(at):
        total = mm(inc_t[at, :], dtwo_b[...]) * (1.0 / KP)
        dpp[at, :] = (total * sg_proc[at, :]).astype(BF)
        gmesh[at, :] = (dtwo[at, :] + mm(dpp[at, :], wpf[...], NT)).astype(BF)

    tiles(third)

    for j in range(3):
        at = jnp.clip(b + j - 1, 0, bands - 1)
        first = pl.multiple_of(lax.rem(at, n_mesh) * shard + at // n_mesh * home, home)
        dwin[j * home:(j + 1) * home, :] = gmesh[pl.ds(first, home), :]
    dpe[...] = (mm(enc_t[...], dwin[...]) * factor * sg_enc[...]).astype(BF)
    weight = mm(gfull[...], dpe[:, mine], TN)
    rs_own[...] = weight
    rs_src[...] = weight.astype(BF)

    def part(index):
        return pl.ds(pl.multiple_of(index * chunk, chunk), chunk)

    scatter, gather = [], []
    for d in range(1, bands):
        to = lax.rem(b + d, bands)
        scatter.append(
            remote(
                rs_src.at[part(to), :], rs_in.at[d - 1], s_rs.at[d - 1], r_rs.at[d - 1],
                **band_at(to),
            )
        )
        scatter[-1].start()
    gwd_ref[...] = mm(two[...], dpd[:, mine], TN).astype(BF)
    gwp_ref[...] = mm(one[...], dpp[:, mine], TN).astype(BF)
    total = rs_own[part(b), :]
    for d in range(1, bands):
        scatter[d - 1].wait_recv()
        total = total + rs_in[d - 1].astype(F32)
    ag[part(b), :] = total.astype(BF)
    for d in range(1, bands):
        gather.append(
            remote(
                ag.at[part(b), :], ag.at[part(b), :], s_ag.at[d - 1], r_ag.at[d - 1],
                **band_at(lax.rem(b + d, bands)),
            )
        )
        gather[-1].start()
    terms = mm(dpe[...], wef[mine, :], NT)
    gg_ref[...] = (cot_ref[...].astype(F32) + terms).astype(BF)
    gm_ref[...] = gmesh[pl.ds(pl.multiple_of(m * shard, shard), shard), mine]
    for copy in wides + indices:
        copy.wait_send()
    halo_sent(0)
    halo_sent(1)
    spread_sent(one, 0)
    spread_sent(ddec, 1)
    for copy in scatter:
        copy.wait_send()
    for d in range(1, bands):
        view = ag.at[part(lax.rem(b + bands - d, bands)), :]
        remote(
            view, view, s_ag.at[d - 1], r_ag.at[d - 1], **band_at(lax.rem(b + d, bands))
        ).wait_recv()
    gwe_ref[...] = ag[...]
    for copy in gather:
        copy.wait_send()


def widen_kernel(*refs):
    for source, target in zip(refs[:5], refs[5:]):
        target[...] = source[...].astype(target.dtype)


def local_fused(
    grid_in, mesh_in, w_enc, w_proc, w_dec, enc_dst, enc_count, dec_src, proc_src, cotangent
):
    n_mesh = lax.axis_size("mesh")
    n_lat = lax.axis_size("lat")
    rows, half = grid_in.shape
    shard = mesh_in.shape[0]
    wide = 2 * half
    home = shard // n_lat
    bands = n_lat * n_mesh
    nodes = shard * n_mesh
    win = 3 * home
    v = pltpu.VMEM
    dma = pltpu.SemaphoreType.DMA
    vmem = pl.BlockSpec(memory_space=pltpu.VMEM)
    shaped = jax.ShapeDtypeStruct
    parts = pl.pallas_call(
        functools.partial(fused_kernel, n_lat, n_mesh),
        out_shape=(
            shaped((rows, half), BF),
            shaped((shard, half), BF),
            shaped((wide, half), BF),
            shaped((wide, half), BF),
            shaped((wide, half), BF),
        ),
        in_specs=[vmem] * 10,
        out_specs=(vmem,) * 5,
        scratch_shapes=[
            v((rows, wide), BF), v((wide, wide), BF), v((wide, wide), BF), v((wide, wide), BF),
            v((8, shard), jnp.int32), v((n_mesh, 8, shard), jnp.int32), v((nodes, 8), F32), v((rows, 8), F32),
            v((win, rows), BF), v((rows, win), BF), v((win, rows), BF),
            v((nodes, nodes), BF), v((nodes, nodes), BF),
            v((4, home, half), BF), v((4, home, half), BF), v((2, home, half), F32),
            v((rows, wide), F32),
            v((nodes, wide), BF), v((nodes, wide), BF), v((nodes, wide), F32),
            v((nodes, wide), BF), v((nodes, wide), BF), v((nodes, wide), BF),
            v((nodes, wide), F32), v((nodes, wide), BF), v((nodes, wide), BF),
            v((nodes, wide), BF), v((rows, wide), BF), v((win, wide), BF),
            v((wide, half), BF), v((wide, half), F32),
            v((bands - 1, wide // bands, half), BF), v((wide, half), BF),
            dma((4,)), dma((4,)), dma((n_mesh - 1,)), dma((n_mesh - 1,)),
            dma((4,)), dma((4,)),
            dma((2, n_lat - 1)), dma((2, n_lat - 1)),
            dma((2, n_lat, n_mesh - 1)), dma((2, n_lat, n_mesh - 1)),
            dma((2, n_lat, n_mesh)), dma((2, n_lat, n_mesh)),
            dma((bands - 1,)), dma((bands - 1,)), dma((bands - 1,)), dma((bands - 1,)),
        ],
        compiler_params=pltpu.CompilerParams(
            collective_id=0, has_side_effects=True, vmem_limit_bytes=56 * 1024 * 1024
        ),
        cost_estimate=pl.CostEstimate(
            flops=10 * nodes * wide * wide, bytes_accessed=8 * rows * wide,
            transcendentals=4 * nodes * wide,
        ),
    )(grid_in, mesh_in, w_enc, w_proc, w_dec, enc_dst.T, enc_count[None, :], dec_src.T, proc_src.T, cotangent)
    return tuple(pl.pallas_call(
        widen_kernel,
        out_shape=(
            shaped((rows, half), BF),
            shaped((shard, half), BF),
            shaped((wide, half), F32),
            shaped((wide, half), F32),
            shaped((wide, half), F32),
        ),
        in_specs=[vmem] * 5,
        out_specs=(vmem,) * 5,
        compiler_params=pltpu.CompilerParams(vmem_limit_bytes=16 * 1024 * 1024),
    )(*parts))


def solution(mesh):
    bands = mesh.shape["lat"] * mesh.shape["mesh"]
    body = local_fused if bands <= 8 and mesh.shape["feat"] == 2 else local_staged
    placed = (
        P(("groups", "lat", "mesh"), "feat"),
        P(("groups", "mesh"), "feat"),
        P(None, "feat"),
        P(None, "feat"),
        P(None, "feat"),
        P(("groups", "lat", "mesh"), None),
        P(("groups", "lat", "mesh")),
        P(("groups", "lat", "mesh"), None),
        P(("groups", "mesh"), None),
        P(("groups", "lat", "mesh"), "feat"),
    )
    return jax.shard_map(
        body,
        mesh=mesh,
        in_specs=placed,
        out_specs=(
            P(("groups", "lat", "mesh"), "feat"),
            P(("groups", "mesh"), "feat"),
            P("groups", "feat"),
            P("groups", "feat"),
            P("groups", "feat"),
        ),
        check_vma=False,
    )
```

```python
import functools

import jax
import jax.numpy as jnp
from jax import lax
from jax.experimental import pallas as pl
from jax.experimental.pallas import tpu as pltpu
from jax.sharding import PartitionSpec as P

KE = 4
KD = 3
KP = 6


def with_halo(value, sides, width):
    for axis, dim in sides:
        size, length = (lax.axis_size(axis), value.shape[dim])
        up = [(i, (i + 1) % size) for i in range(size - 1)]
        down = [(j, i) for i, j in up]
        last = lax.slice_in_dim(value, length - width, length, axis=dim)
        first = lax.slice_in_dim(value, 0, width, axis=dim)
        before = lax.ppermute(last, axis, up)
        after = lax.ppermute(first, axis, down)
        value = jnp.concatenate([before, value, after], axis=dim)
    return value


def silu_grad(pre):
    sig = jax.nn.sigmoid(pre)
    return sig * (1.0 + pre * (1.0 - sig))


def window_slots(targets, is_valid, shard_rows, home_rows, n_mesh, band_index):
    owner_shard = targets // shard_rows
    inner_row = targets % shard_rows
    home_id = inner_row // home_rows * n_mesh + owner_shard
    slot_ids = (home_id - band_index + 1) * home_rows + inner_row % home_rows
    return jnp.where(is_valid, slot_ids, -1)


def window_matrix(slot_ids, win_rows):
    row_ids = jnp.arange(win_rows, dtype=jnp.int32)[:, None]
    matrix = jnp.zeros((win_rows, slot_ids.shape[0]), jnp.bfloat16)
    for column in range(slot_ids.shape[1]):
        matrix = matrix + (row_ids == slot_ids[:, column][None, :]).astype(jnp.bfloat16)
    return matrix


def band_sum(window, home_rows):
    stacked = window.reshape(3, home_rows, window.shape[1])
    padded_win = with_halo(stacked.astype(jnp.bfloat16), ((("lat", "mesh"), 0),), 3).astype(
        stacked.dtype
    )
    return padded_win[2] + padded_win[4] + padded_win[6]


def collect_rows(home_block):
    return lax.all_gather(home_block, "lat", axis=0, tiled=True)


def widen(latent):
    return lax.all_gather(latent, "feat", axis=1, tiled=True)


def back_product(d_pre, weight):
    return lax.dot_general(
        d_pre, weight, (((1,), (1,)), ((), ())), preferred_element_type=jnp.float32
    )


def mesh_back(d_pre, weight):
    return lax.psum_scatter(
        back_product(d_pre, weight).astype(jnp.bfloat16), "feat", scatter_dimension=1, tiled=True
    ).astype(jnp.float32)


def contract_rows(left_rows, right_rows):
    return lax.dot_general(
        left_rows, right_rows, (((0,), (0,)), ((), ())), preferred_element_type=jnp.float32
    )


def local_staged(grid_in, mesh_in, w_enc, w_proc, w_dec, enc_dst, enc_count, dec_src, proc_src, cotangent):
    n_mesh = lax.axis_size("mesh")
    n_lat = lax.axis_size("lat")
    shard_rows = mesh_in.shape[0]
    home_rows = shard_rows // n_lat
    grid_rows = grid_in.shape[0]
    enc_factor = home_rows / grid_rows
    band_index = lax.axis_index("lat") * n_mesh + lax.axis_index("mesh")
    home_first = lax.axis_index("lat") * home_rows
    win_rows = 3 * home_rows
    enc_valid = jnp.arange(KE, dtype=jnp.int32)[None, :] < enc_count[:, None]
    enc_matrix = window_matrix(
        window_slots(enc_dst, enc_valid, shard_rows, home_rows, n_mesh, band_index), win_rows
    )
    dec_valid = jnp.ones(dec_src.shape, jnp.bool_)
    dec_matrix = window_matrix(
        window_slots(dec_src, dec_valid, shard_rows, home_rows, n_mesh, band_index), win_rows
    )
    grid_full = lax.all_gather(grid_in, "feat", axis=1, tiled=True)
    pre_enc = jnp.dot(grid_full, w_enc, preferred_element_type=jnp.float32)
    enc_msg = jax.nn.silu(pre_enc).astype(jnp.bfloat16)
    enc_window = jnp.dot(enc_matrix, enc_msg, preferred_element_type=jnp.float32) * enc_factor
    aggregate_home = band_sum(enc_window, home_rows)
    mesh_home = lax.dynamic_slice_in_dim(mesh_in, home_first, home_rows, 0)
    latent_one = collect_rows((mesh_home.astype(jnp.float32) + aggregate_home).astype(jnp.bfloat16))
    one_full = widen(latent_one)
    pre_proc = jnp.dot(one_full, w_proc, preferred_element_type=jnp.float32)
    proc_msg = jax.nn.silu(pre_proc).astype(jnp.bfloat16)

    def incidence(row_count):
        node_ids = jnp.arange(row_count, dtype=jnp.int32)
        matrix = jnp.zeros((shard_rows, row_count), jnp.bfloat16)
        for column in range(KP):
            matrix = matrix + (proc_src[:, column][:, None] == node_ids[None, :]).astype(
                jnp.bfloat16
            )
        return matrix

    shard_piece = lax.all_gather(proc_msg, "mesh", axis=0, tiled=True)
    neighbour_sum = jnp.dot(
        incidence(shard_piece.shape[0]), shard_piece, preferred_element_type=jnp.float32
    )
    latent_two = (latent_one.astype(jnp.float32) + neighbour_sum / KP).astype(jnp.bfloat16)
    two_full = widen(latent_two)
    pre_dec = jnp.dot(two_full, w_dec, preferred_element_type=jnp.float32)
    dec_window = jnp.dot(dec_matrix, cotangent, preferred_element_type=jnp.float32) / KD
    d_dec = collect_rows(band_sum(dec_window, home_rows).astype(jnp.bfloat16))
    d_pre_dec = (d_dec.astype(jnp.float32) * silu_grad(pre_dec)).astype(jnp.bfloat16)
    d_two = mesh_back(d_pre_dec, w_dec)
    d_two_b = d_two.astype(jnp.bfloat16)
    d_proc = (
        lax.psum_scatter(
            contract_rows(incidence(shard_rows * lax.axis_size("mesh")), d_two_b).astype(
                jnp.bfloat16
            ),
            "mesh",
            scatter_dimension=0,
            tiled=True,
        ).astype(jnp.float32)
        / KP
    )
    d_pre_proc = (d_proc * silu_grad(pre_proc)).astype(jnp.bfloat16)
    d_one = d_two + mesh_back(d_pre_proc, w_proc)
    grad_mesh = d_one.astype(jnp.bfloat16)
    grad_home = lax.dynamic_slice_in_dim(grad_mesh, home_first, home_rows, 0)
    mesh_window = with_halo(grad_home, ((("lat", "mesh"), 0),), home_rows)
    d_enc = contract_rows(enc_matrix, mesh_window) * enc_factor
    d_pre_enc = (d_enc * silu_grad(pre_enc)).astype(jnp.bfloat16)
    grid_terms = lax.psum_scatter(
        back_product(d_pre_enc, w_enc).astype(jnp.bfloat16), "feat", scatter_dimension=1, tiled=True
    ).astype(jnp.float32)
    grad_grid = (cotangent.astype(jnp.float32) + grid_terms).astype(jnp.bfloat16)
    enc_term = contract_rows(grid_full, d_pre_enc)
    grad_w_proc, grad_w_dec = (
        lax.psum(contract_rows(one_full, d_pre_proc).astype(jnp.bfloat16), "mesh").astype(
            jnp.float32
        ),
        lax.psum(contract_rows(two_full, d_pre_dec).astype(jnp.bfloat16), "mesh").astype(
            jnp.float32
        ),
    )
    grad_w_enc = lax.psum(enc_term, ("lat", "mesh"))
    return (grad_grid, grad_mesh, grad_w_enc, grad_w_proc, grad_w_dec)


BF = jnp.bfloat16
F32 = jnp.float32
NN = (((1,), (0,)), ((), ()))
NT = (((1,), (1,)), ((), ()))
TN = (((0,), (0,)), ((), ()))


def mm(left, right, dims=NN):
    return lax.dot_general(left, right, dims, preferred_element_type=F32)


def sigm(value):
    return 1.0 / (1.0 + jnp.exp(-value))


def fused_kernel(
    n_lat, n_mesh,
    grid_hbm, mesh_hbm, we_hbm, wp_hbm, wd_hbm, dst_ref, count_ref, src_ref, pi_ref, cot_hbm,
    gg_hbm, gm_hbm, gwe_hbm, gwp_hbm, gwd_hbm,
    mesh_ref, cot_ref, gg_ref, gwp_ref, gwd_ref, s_in, s_out,
    gfull, wef, wpf, wdf, stage, psall, pst, idt, enc_m, enc_t, dec_m, inc_a, inc_t,
    halo_out, halo_in, own_win, sg_enc, one, ddec, sg_proc, pmsg, two, dpd, dtwo, dtwo_b, dpp,
    gmesh, dpe, dwin, rs_src, rs_own, rs_in, ag,
    s_f, r_f, s_p, r_p, s_h, r_h, s_z, r_z, s_x, r_x, s_c, r_c, s_rs, r_rs, s_ag, r_ag,
):
    rows, half = cot_ref.shape
    shard = mesh_ref.shape[0]
    home = shard // n_lat
    bands = n_lat * n_mesh
    nodes = shard * n_mesh
    wide = 2 * half
    chunk = wide // bands
    win = 3 * home
    factor = home / rows
    l = lax.axis_index("lat")
    m = lax.axis_index("mesh")
    f = lax.axis_index("feat")
    b = l * n_mesh + m
    mine = pl.ds(pl.multiple_of(f * half, half), half)

    def remote(source, target, send, recv, **where):
        return pltpu.make_async_remote_copy(
            src_ref=source, dst_ref=target, send_sem=send, recv_sem=recv,
            device_id=where, device_id_type=pl.DeviceIdType.MESH,
        )

    def band_at(index):
        return {"lat": index // n_mesh, "mesh": lax.rem(index, n_mesh)}

    loads = [
        pltpu.make_async_copy(s, t, s_in.at[i])
        for i, (s, t) in enumerate(
            (
                (cot_hbm, cot_ref), (grid_hbm, gfull.at[:, mine]), (we_hbm, wef.at[:, mine]),
                (mesh_hbm, mesh_ref), (wp_hbm, wpf.at[:, mine]), (wd_hbm, wdf.at[:, mine]),
            )
        )
    ]
    for copy in loads:
        copy.start()
    barrier = pltpu.get_barrier_semaphore()
    for d in range(1, bands):
        pl.semaphore_signal(
            barrier, inc=1, device_id=band_at(lax.rem(b + d, bands)),
            device_id_type=pl.DeviceIdType.MESH,
        )
    pl.semaphore_signal(
        barrier, inc=1, device_id={"feat": 1 - f}, device_id_type=pl.DeviceIdType.MESH
    )

    def slots(raw):
        inner = raw & (shard - 1)
        home_id = (inner >> (home.bit_length() - 1)) * n_mesh + (raw >> (shard.bit_length() - 1))
        return (home_id - b + 1) * home + (inner & (home - 1))

    order = lax.broadcasted_iota(jnp.int32, dst_ref.shape, 0)
    enc_ids = jnp.where(order < count_ref[...], slots(dst_ref[...]), -1)
    dec_ids = slots(src_ref[...])
    idt[...] = jnp.concatenate([enc_ids, enc_ids], axis=0).astype(F32).T
    stage[0:KP, :] = pi_ref[...]
    stage[KP:8, :] = jnp.zeros((8 - KP, shard), jnp.int32)

    def one_hot(target, ids):
        step = 64
        for r in range(0, win, step):
            node = lax.broadcasted_iota(jnp.int32, (step, rows), 0) + r
            acc = jnp.zeros((step, rows), F32)
            for k in range(ids.shape[0]):
                acc = acc + jnp.where(node == ids[k:k + 1, :], 1.0, 0.0)
            target[r:r + step, :] = acc.astype(BF)

    one_hot(dec_m, dec_ids)
    loads[0].wait()
    dec_win = mm(dec_m[...], cot_ref[...]) / KD
    halo_out[0] = dec_win[2 * home:, :].astype(BF)
    halo_out[1] = dec_win[:home, :].astype(BF)
    own_win[0] = dec_win[home:2 * home, :]
    one_hot(enc_m, enc_ids)
    psall[m] = stage[...]

    @pl.when(b == 0)
    def _():
        halo_in[0] = jnp.zeros((home, half), BF)
        halo_in[2] = jnp.zeros((home, half), BF)

    @pl.when(b == bands - 1)
    def _():
        halo_in[1] = jnp.zeros((home, half), BF)
        halo_in[3] = jnp.zeros((home, half), BF)

    for copy in loads[1:]:
        copy.wait()
    pl.semaphore_wait(barrier, bands)

    wides = [
        remote(t.at[:, mine], t.at[:, mine], s_f.at[i], r_f.at[i], feat=1 - f)
        for i, t in enumerate((gfull, wef, wpf, wdf))
    ]
    indices = [
        remote(stage, psall.at[m], s_p.at[e - 1], r_p.at[e - 1], mesh=lax.rem(m + e, n_mesh))
        for e in range(1, n_mesh)
    ]
    wides[0].start()

    def halo(i, up):
        slot = 2 * i + (0 if up else 1)
        return remote(
            halo_out.at[slot], halo_in.at[slot], s_h.at[slot], r_h.at[slot],
            **band_at(b + 1 if up else b - 1),
        )

    def halo_start(i):
        @pl.when(b < bands - 1)
        def _():
            halo(i, True).start()

        @pl.when(b > 0)
        def _():
            halo(i, False).start()

    def halo_recv(i):
        @pl.when(b > 0)
        def _():
            halo(i, True).wait_recv()

        @pl.when(b < bands - 1)
        def _():
            halo(i, False).wait_recv()

    def halo_sent(i):
        @pl.when(b < bands - 1)
        def _():
            halo(i, True).wait_send()

        @pl.when(b > 0)
        def _():
            halo(i, False).wait_send()

    halo_start(0)
    for copy in indices:
        copy.start()

    wides[0].wait_recv()
    for copy in wides[1:]:
        copy.start()
    pre = mm(gfull[...], wef[:, mine])
    enc_win = mm(enc_m[...], (pre * sigm(pre)).astype(BF)) * factor
    halo_out[2] = enc_win[2 * home:, :].astype(BF)
    halo_out[3] = enc_win[:home, :].astype(BF)
    own_win[1] = enc_win[home:2 * home, :]
    halo_start(1)

    for copy in indices:
        copy.wait_recv()
    step = 64
    for i in range(n_mesh):
        pst[i * shard:(i + 1) * shard, :] = psall[i].astype(F32).T

    def build_a(t, carry):
        r = pl.multiple_of(t * step, step)
        node = lax.broadcasted_iota(jnp.int32, (step, nodes), 1).astype(F32)
        acc = jnp.zeros((step, nodes), F32)
        for k in range(KP):
            acc = acc + jnp.where(node == pst[pl.ds(r, step), k:k + 1], 1.0, 0.0)
        inc_a[pl.ds(r, step), :] = acc.astype(BF)
        return carry

    def build_t(t, carry):
        r = pl.multiple_of(t * step, step)
        for i in range(n_mesh):
            node = lax.broadcasted_iota(jnp.int32, (step, shard), 0) + r
            acc = jnp.zeros((step, shard), F32)
            for k in range(KP):
                acc = acc + jnp.where(node == psall[i, k:k + 1, :], 1.0, 0.0)
            inc_t[pl.ds(r, step), i * shard:(i + 1) * shard] = acc.astype(BF)
        return carry

    def build_e(t, carry):
        r = pl.multiple_of(t * step, step)
        node = lax.broadcasted_iota(jnp.int32, (step, win), 1).astype(F32)
        acc = jnp.zeros((step, win), F32)
        for k in range(KE):
            acc = acc + jnp.where(node == idt[pl.ds(r, step), k:k + 1], 1.0, 0.0)
        enc_t[pl.ds(r, step), :] = acc.astype(BF)
        return carry

    def block(array, d, e):
        at_l = lax.rem(l + n_lat - d, n_lat)
        at_m = lax.rem(m + n_mesh - e, n_mesh)
        return array.at[pl.ds(pl.multiple_of(at_m * shard + at_l * home, home), home), mine]

    def along_lat(array, a, d):
        own = block(array, 0, 0)
        return remote(own, own, s_z.at[a, d - 1], r_z.at[a, d - 1], lat=lax.rem(l + d, n_lat))

    def recv_lat(array, a, d):
        view = block(array, d, 0)
        return remote(view, view, s_z.at[a, d - 1], r_z.at[a, d - 1], lat=lax.rem(l + d, n_lat))

    def along_mesh(array, a, d, e):
        view = block(array, d, 0)
        return remote(
            view, view, s_x.at[a, d, e - 1], r_x.at[a, d, e - 1], mesh=lax.rem(m + e, n_mesh)
        )

    def recv_mesh(array, a, d, e):
        view = block(array, d, e)
        return remote(
            view, view, s_x.at[a, d, e - 1], r_x.at[a, d, e - 1], mesh=lax.rem(m + e, n_mesh)
        )

    def along_feat(array, a, d, e):
        view = block(array, d, e)
        return remote(view, view, s_c.at[a, d, e], r_c.at[a, d, e], feat=1 - f)

    def spread_own(array, a):
        for e in range(1, n_mesh):
            along_mesh(array, a, 0, e).start()
        for d in range(1, n_lat):
            along_lat(array, a, d).start()
        along_feat(array, a, 0, 0).start()

    def spread_lat(array, a):
        for d in range(1, n_lat):
            recv_lat(array, a, d).wait_recv()
            for e in range(1, n_mesh):
                along_mesh(array, a, d, e).start()
            along_feat(array, a, d, 0).start()

    def spread_mesh(array, a):
        for d in range(n_lat):
            for e in range(1, n_mesh):
                recv_mesh(array, a, d, e).wait_recv()
                along_feat(array, a, d, e).start()

    def spread_done(array, a):
        for d in range(n_lat):
            for e in range(n_mesh):
                along_feat(array, a, d, e).wait_recv()

    def spread_sent(array, a):
        for d in range(1, n_lat):
            along_lat(array, a, d).wait_send()
        for d in range(n_lat):
            for e in range(n_mesh):
                if e:
                    along_mesh(array, a, d, e).wait_send()
                along_feat(array, a, d, e).wait_send()

    def banded(i):
        return own_win[i] + halo_in[2 * i].astype(F32) + halo_in[2 * i + 1].astype(F32)

    home_rows = pl.ds(pl.multiple_of(m * shard + l * home, home), home)
    halo_recv(0)
    ddec[home_rows, mine] = banded(0).astype(BF)
    spread_own(ddec, 1)
    lax.fori_loop(0, rows // step, build_e, 0)
    halo_recv(1)
    mesh_home = mesh_ref[pl.ds(pl.multiple_of(l * home, home), home), :].astype(F32)
    one[home_rows, mine] = (mesh_home + banded(1)).astype(BF)
    spread_own(one, 0)
    lax.fori_loop(0, nodes // step, build_a, 0)
    spread_lat(one, 0)
    spread_lat(ddec, 1)
    spread_mesh(one, 0)
    lax.fori_loop(0, nodes // step, build_t, 0)
    wides[1].wait_recv()
    wides[2].wait_recv()
    wides[3].wait_recv()
    tile = min(512, nodes)
    spread_done(one, 0)

    def tiles(body):
        for r in range(0, nodes, tile):
            body(slice(r, r + tile))

    def proc(at):
        value = mm(one[at, :], wpf[...])
        sig = sigm(value)
        pmsg[at, :] = (value * sig).astype(BF)
        sg_proc[at, :] = sig * (1.0 + value * (1.0 - sig))

    tiles(proc)
    spread_mesh(ddec, 1)

    def second(at):
        total = mm(inc_a[at, :], pmsg[...])
        two[at, :] = (one[at, :].astype(F32) + total * (1.0 / KP)).astype(BF)

    tiles(second)

    pre_all = mm(gfull[...], wef[...])
    sig_all = sigm(pre_all)
    sg_enc[...] = sig_all * (1.0 + pre_all * (1.0 - sig_all))
    spread_done(ddec, 1)

    def decode(at):
        value = mm(two[at, :], wdf[...])
        sig = sigm(value)
        grad = sig * (1.0 + value * (1.0 - sig))
        dpd[at, :] = (ddec[at, :].astype(F32) * grad).astype(BF)
        back = mm(dpd[at, :], wdf[...], NT)
        dtwo[at, :] = back
        dtwo_b[at, :] = back.astype(BF)

    tiles(decode)

    def third(at):
        total = mm(inc_t[at, :], dtwo_b[...]) * (1.0 / KP)
        dpp[at, :] = (total * sg_proc[at, :]).astype(BF)
        gmesh[at, :] = (dtwo[at, :] + mm(dpp[at, :], wpf[...], NT)).astype(BF)

    tiles(third)

    def store(i, source, target):
        copy = pltpu.make_async_copy(source, target, s_out.at[i])
        copy.start()
        return copy

    own_rows = pl.ds(pl.multiple_of(m * shard, shard), shard)
    stores = [store(0, gmesh.at[own_rows, mine], gm_hbm)]
    for j in range(3):
        at = jnp.clip(b + j - 1, 0, bands - 1)
        first = pl.multiple_of(lax.rem(at, n_mesh) * shard + at // n_mesh * home, home)
        dwin[j * home:(j + 1) * home, :] = gmesh[pl.ds(first, home), :]
    dpe[...] = (mm(enc_t[...], dwin[...]) * factor * sg_enc[...]).astype(BF)
    weight = mm(gfull[...], dpe[:, mine], TN)
    rs_own[...] = weight
    rs_src[...] = weight.astype(BF)

    def part(index):
        return pl.ds(pl.multiple_of(index * chunk, chunk), chunk)

    scatter, gather = [], []
    for d in range(1, bands):
        to = lax.rem(b + d, bands)
        scatter.append(
            remote(
                rs_src.at[part(to), :], rs_in.at[d - 1], s_rs.at[d - 1], r_rs.at[d - 1],
                **band_at(to),
            )
        )
        scatter[-1].start()
    gwd_ref[...] = mm(two[...], dpd[:, mine], TN).astype(BF)
    stores.append(store(1, gwd_ref, gwd_hbm))
    gwp_ref[...] = mm(one[...], dpp[:, mine], TN).astype(BF)
    stores.append(store(2, gwp_ref, gwp_hbm))
    total = rs_own[part(b), :]
    for d in range(1, bands):
        scatter[d - 1].wait_recv()
        total = total + rs_in[d - 1].astype(F32)
    ag[part(b), :] = total.astype(BF)
    for d in range(1, bands):
        gather.append(
            remote(
                ag.at[part(b), :], ag.at[part(b), :], s_ag.at[d - 1], r_ag.at[d - 1],
                **band_at(lax.rem(b + d, bands)),
            )
        )
        gather[-1].start()
    terms = mm(dpe[...], wef[mine, :], NT)
    gg_ref[...] = (cot_ref[...].astype(F32) + terms).astype(BF)
    stores.append(store(3, gg_ref, gg_hbm))
    for copy in wides + indices:
        copy.wait_send()
    halo_sent(0)
    halo_sent(1)
    spread_sent(one, 0)
    spread_sent(ddec, 1)
    for copy in scatter:
        copy.wait_send()
    for d in range(1, bands):
        view = ag.at[part(lax.rem(b + bands - d, bands)), :]
        remote(
            view, view, s_ag.at[d - 1], r_ag.at[d - 1], **band_at(lax.rem(b + d, bands))
        ).wait_recv()
    stores.append(store(4, ag, gwe_hbm))
    for copy in gather:
        copy.wait_send()
    for copy in stores:
        copy.wait()


def widen_kernel(*refs):
    for source, target in zip(refs[:5], refs[5:]):
        target[...] = source[...].astype(target.dtype)


def local_fused(
    grid_in, mesh_in, w_enc, w_proc, w_dec, enc_dst, enc_count, dec_src, proc_src, cotangent
):
    n_mesh = lax.axis_size("mesh")
    n_lat = lax.axis_size("lat")
    rows, half = grid_in.shape
    shard = mesh_in.shape[0]
    wide = 2 * half
    home = shard // n_lat
    bands = n_lat * n_mesh
    nodes = shard * n_mesh
    win = 3 * home
    v = pltpu.VMEM
    dma = pltpu.SemaphoreType.DMA
    vmem = pl.BlockSpec(memory_space=pltpu.VMEM)
    hbm = pl.BlockSpec(memory_space=pl.ANY)
    shaped = jax.ShapeDtypeStruct
    parts = pl.pallas_call(
        functools.partial(fused_kernel, n_lat, n_mesh),
        out_shape=(
            shaped((rows, half), BF),
            shaped((shard, half), BF),
            shaped((wide, half), BF),
            shaped((wide, half), BF),
            shaped((wide, half), BF),
        ),
        in_specs=[hbm] * 5 + [vmem] * 4 + [hbm],
        out_specs=(hbm,) * 5,
        scratch_shapes=[
            v((shard, half), BF), v((rows, half), BF), v((rows, half), BF), v((wide, half), BF),
            v((wide, half), BF), dma((6,)), dma((5,)),
            v((rows, wide), BF), v((wide, wide), BF), v((wide, wide), BF), v((wide, wide), BF),
            v((8, shard), jnp.int32), v((n_mesh, 8, shard), jnp.int32), v((nodes, 8), F32), v((rows, 8), F32),
            v((win, rows), BF), v((rows, win), BF), v((win, rows), BF),
            v((nodes, nodes), BF), v((nodes, nodes), BF),
            v((4, home, half), BF), v((4, home, half), BF), v((2, home, half), F32),
            v((rows, wide), F32),
            v((nodes, wide), BF), v((nodes, wide), BF), v((nodes, wide), F32),
            v((nodes, wide), BF), v((nodes, wide), BF), v((nodes, wide), BF),
            v((nodes, wide), F32), v((nodes, wide), BF), v((nodes, wide), BF),
            v((nodes, wide), BF), v((rows, wide), BF), v((win, wide), BF),
            v((wide, half), BF), v((wide, half), F32),
            v((bands - 1, wide // bands, half), BF), v((wide, half), BF),
            dma((4,)), dma((4,)), dma((n_mesh - 1,)), dma((n_mesh - 1,)),
            dma((4,)), dma((4,)),
            dma((2, n_lat - 1)), dma((2, n_lat - 1)),
            dma((2, n_lat, n_mesh - 1)), dma((2, n_lat, n_mesh - 1)),
            dma((2, n_lat, n_mesh)), dma((2, n_lat, n_mesh)),
            dma((bands - 1,)), dma((bands - 1,)), dma((bands - 1,)), dma((bands - 1,)),
        ],
        compiler_params=pltpu.CompilerParams(
            collective_id=0, has_side_effects=True, vmem_limit_bytes=56 * 1024 * 1024
        ),
        cost_estimate=pl.CostEstimate(
            flops=10 * nodes * wide * wide, bytes_accessed=8 * rows * wide,
            transcendentals=4 * nodes * wide,
        ),
    )(grid_in, mesh_in, w_enc, w_proc, w_dec, enc_dst.T, enc_count[None, :], dec_src.T, proc_src.T, cotangent)
    return tuple(pl.pallas_call(
        widen_kernel,
        out_shape=(
            shaped((rows, half), BF),
            shaped((shard, half), BF),
            shaped((wide, half), F32),
            shaped((wide, half), F32),
            shaped((wide, half), F32),
        ),
        in_specs=[vmem] * 5,
        out_specs=(vmem,) * 5,
        compiler_params=pltpu.CompilerParams(vmem_limit_bytes=60 * 1024 * 1024),
    )(*parts))


def solution(mesh):
    bands = mesh.shape["lat"] * mesh.shape["mesh"]
    body = local_fused if bands <= 8 and mesh.shape["feat"] == 2 else local_staged
    placed = (
        P(("groups", "lat", "mesh"), "feat"),
        P(("groups", "mesh"), "feat"),
        P(None, "feat"),
        P(None, "feat"),
        P(None, "feat"),
        P(("groups", "lat", "mesh"), None),
        P(("groups", "lat", "mesh")),
        P(("groups", "lat", "mesh"), None),
        P(("groups", "mesh"), None),
        P(("groups", "lat", "mesh"), "feat"),
    )
    return jax.shard_map(
        body,
        mesh=mesh,
        in_specs=placed,
        out_specs=(
            P(("groups", "lat", "mesh"), "feat"),
            P(("groups", "mesh"), "feat"),
            P("groups", "feat"),
            P("groups", "feat"),
            P("groups", "feat"),
        ),
        check_vma=False,
    )
```

```python
import functools

import jax
import jax.numpy as jnp
from jax import lax
from jax.experimental import pallas as pl
from jax.experimental.pallas import tpu as pltpu
from jax.sharding import PartitionSpec as P

KE = 4
KD = 3
KP = 6


def with_halo(value, sides, width):
    for axis, dim in sides:
        size, length = (lax.axis_size(axis), value.shape[dim])
        up = [(i, (i + 1) % size) for i in range(size - 1)]
        down = [(j, i) for i, j in up]
        last = lax.slice_in_dim(value, length - width, length, axis=dim)
        first = lax.slice_in_dim(value, 0, width, axis=dim)
        before = lax.ppermute(last, axis, up)
        after = lax.ppermute(first, axis, down)
        value = jnp.concatenate([before, value, after], axis=dim)
    return value


def silu_grad(pre):
    sig = jax.nn.sigmoid(pre)
    return sig * (1.0 + pre * (1.0 - sig))


def window_slots(targets, is_valid, shard_rows, home_rows, n_mesh, band_index):
    owner_shard = targets // shard_rows
    inner_row = targets % shard_rows
    home_id = inner_row // home_rows * n_mesh + owner_shard
    slot_ids = (home_id - band_index + 1) * home_rows + inner_row % home_rows
    return jnp.where(is_valid, slot_ids, -1)


def window_matrix(slot_ids, win_rows):
    row_ids = jnp.arange(win_rows, dtype=jnp.int32)[:, None]
    matrix = jnp.zeros((win_rows, slot_ids.shape[0]), jnp.bfloat16)
    for column in range(slot_ids.shape[1]):
        matrix = matrix + (row_ids == slot_ids[:, column][None, :]).astype(jnp.bfloat16)
    return matrix


def band_sum(window, home_rows):
    stacked = window.reshape(3, home_rows, window.shape[1])
    padded_win = with_halo(stacked.astype(jnp.bfloat16), ((("lat", "mesh"), 0),), 3).astype(
        stacked.dtype
    )
    return padded_win[2] + padded_win[4] + padded_win[6]


def collect_rows(home_block):
    return lax.all_gather(home_block, "lat", axis=0, tiled=True)


def widen(latent):
    return lax.all_gather(latent, "feat", axis=1, tiled=True)


def back_product(d_pre, weight):
    return lax.dot_general(
        d_pre, weight, (((1,), (1,)), ((), ())), preferred_element_type=jnp.float32
    )


def mesh_back(d_pre, weight):
    return lax.psum_scatter(
        back_product(d_pre, weight).astype(jnp.bfloat16), "feat", scatter_dimension=1, tiled=True
    ).astype(jnp.float32)


def contract_rows(left_rows, right_rows):
    return lax.dot_general(
        left_rows, right_rows, (((0,), (0,)), ((), ())), preferred_element_type=jnp.float32
    )


def local_staged(grid_in, mesh_in, w_enc, w_proc, w_dec, enc_dst, enc_count, dec_src, proc_src, cotangent):
    n_mesh = lax.axis_size("mesh")
    n_lat = lax.axis_size("lat")
    shard_rows = mesh_in.shape[0]
    home_rows = shard_rows // n_lat
    grid_rows = grid_in.shape[0]
    enc_factor = home_rows / grid_rows
    band_index = lax.axis_index("lat") * n_mesh + lax.axis_index("mesh")
    home_first = lax.axis_index("lat") * home_rows
    win_rows = 3 * home_rows
    enc_valid = jnp.arange(KE, dtype=jnp.int32)[None, :] < enc_count[:, None]
    enc_matrix = window_matrix(
        window_slots(enc_dst, enc_valid, shard_rows, home_rows, n_mesh, band_index), win_rows
    )
    dec_valid = jnp.ones(dec_src.shape, jnp.bool_)
    dec_matrix = window_matrix(
        window_slots(dec_src, dec_valid, shard_rows, home_rows, n_mesh, band_index), win_rows
    )
    grid_full = lax.all_gather(grid_in, "feat", axis=1, tiled=True)
    pre_enc = jnp.dot(grid_full, w_enc, preferred_element_type=jnp.float32)
    enc_msg = jax.nn.silu(pre_enc).astype(jnp.bfloat16)
    enc_window = jnp.dot(enc_matrix, enc_msg, preferred_element_type=jnp.float32) * enc_factor
    aggregate_home = band_sum(enc_window, home_rows)
    mesh_home = lax.dynamic_slice_in_dim(mesh_in, home_first, home_rows, 0)
    latent_one = collect_rows((mesh_home.astype(jnp.float32) + aggregate_home).astype(jnp.bfloat16))
    one_full = widen(latent_one)
    pre_proc = jnp.dot(one_full, w_proc, preferred_element_type=jnp.float32)
    proc_msg = jax.nn.silu(pre_proc).astype(jnp.bfloat16)

    def incidence(row_count):
        node_ids = jnp.arange(row_count, dtype=jnp.int32)
        matrix = jnp.zeros((shard_rows, row_count), jnp.bfloat16)
        for column in range(KP):
            matrix = matrix + (proc_src[:, column][:, None] == node_ids[None, :]).astype(
                jnp.bfloat16
            )
        return matrix

    shard_piece = lax.all_gather(proc_msg, "mesh", axis=0, tiled=True)
    neighbour_sum = jnp.dot(
        incidence(shard_piece.shape[0]), shard_piece, preferred_element_type=jnp.float32
    )
    latent_two = (latent_one.astype(jnp.float32) + neighbour_sum / KP).astype(jnp.bfloat16)
    two_full = widen(latent_two)
    pre_dec = jnp.dot(two_full, w_dec, preferred_element_type=jnp.float32)
    dec_window = jnp.dot(dec_matrix, cotangent, preferred_element_type=jnp.float32) / KD
    d_dec = collect_rows(band_sum(dec_window, home_rows).astype(jnp.bfloat16))
    d_pre_dec = (d_dec.astype(jnp.float32) * silu_grad(pre_dec)).astype(jnp.bfloat16)
    d_two = mesh_back(d_pre_dec, w_dec)
    d_two_b = d_two.astype(jnp.bfloat16)
    d_proc = (
        lax.psum_scatter(
            contract_rows(incidence(shard_rows * lax.axis_size("mesh")), d_two_b).astype(
                jnp.bfloat16
            ),
            "mesh",
            scatter_dimension=0,
            tiled=True,
        ).astype(jnp.float32)
        / KP
    )
    d_pre_proc = (d_proc * silu_grad(pre_proc)).astype(jnp.bfloat16)
    d_one = d_two + mesh_back(d_pre_proc, w_proc)
    grad_mesh = d_one.astype(jnp.bfloat16)
    grad_home = lax.dynamic_slice_in_dim(grad_mesh, home_first, home_rows, 0)
    mesh_window = with_halo(grad_home, ((("lat", "mesh"), 0),), home_rows)
    d_enc = contract_rows(enc_matrix, mesh_window) * enc_factor
    d_pre_enc = (d_enc * silu_grad(pre_enc)).astype(jnp.bfloat16)
    grid_terms = lax.psum_scatter(
        back_product(d_pre_enc, w_enc).astype(jnp.bfloat16), "feat", scatter_dimension=1, tiled=True
    ).astype(jnp.float32)
    grad_grid = (cotangent.astype(jnp.float32) + grid_terms).astype(jnp.bfloat16)
    enc_term = contract_rows(grid_full, d_pre_enc)
    grad_w_proc, grad_w_dec = (
        lax.psum(contract_rows(one_full, d_pre_proc).astype(jnp.bfloat16), "mesh").astype(
            jnp.float32
        ),
        lax.psum(contract_rows(two_full, d_pre_dec).astype(jnp.bfloat16), "mesh").astype(
            jnp.float32
        ),
    )
    grad_w_enc = lax.psum(enc_term, ("lat", "mesh"))
    return (grad_grid, grad_mesh, grad_w_enc, grad_w_proc, grad_w_dec)


BF = jnp.bfloat16
F32 = jnp.float32
NN = (((1,), (0,)), ((), ()))
NT = (((1,), (1,)), ((), ()))
TN = (((0,), (0,)), ((), ()))


def mm(left, right, dims=NN):
    return lax.dot_general(left, right, dims, preferred_element_type=F32)


def sigm(value):
    return 1.0 / (1.0 + jnp.exp(-value))


def fused_kernel(
    n_lat, n_mesh,
    grid_hbm, mesh_hbm, we_hbm, wp_hbm, wd_hbm, dst_ref, count_ref, src_ref, pi_ref, cot_hbm,
    gg_hbm, gm_hbm, gwe_hbm, gwp_hbm, gwd_hbm,
    mesh_ref, cot_ref, gg_ref, gwp_ref, gwd_ref, s_in, s_out,
    gfull, wef, wpf, wdf, stage, psall, pst, idt, enc_m, enc_t, dec_m, inc_a, inc_t,
    halo_out, halo_in, own_win, sg_enc, one, ddec, sg_proc, pmsg, two, dpd, dtwo, dtwo_b, dpp,
    gmesh, dpe, dwin, rs_src, rs_own, rs_x, rs_out, rs_in, ag,
    s_f, r_f, s_p, r_p, s_h, r_h, s_z, r_z, s_x, r_x, s_c, r_c, s_rx, r_rx, s_rs, r_rs, s_ag, r_ag, s_ax, r_ax,
):
    rows, half = cot_ref.shape
    shard = mesh_ref.shape[0]
    home = shard // n_lat
    bands = n_lat * n_mesh
    nodes = shard * n_mesh
    wide = 2 * half
    chunk = wide // bands
    win = 3 * home
    factor = home / rows
    l = lax.axis_index("lat")
    m = lax.axis_index("mesh")
    f = lax.axis_index("feat")
    b = l * n_mesh + m
    mine = pl.ds(pl.multiple_of(f * half, half), half)

    def remote(source, target, send, recv, **where):
        return pltpu.make_async_remote_copy(
            src_ref=source, dst_ref=target, send_sem=send, recv_sem=recv,
            device_id=where, device_id_type=pl.DeviceIdType.MESH,
        )

    def band_at(index):
        return {"lat": index // n_mesh, "mesh": lax.rem(index, n_mesh)}

    loads = [
        pltpu.make_async_copy(s, t, s_in.at[i])
        for i, (s, t) in enumerate(
            (
                (cot_hbm, cot_ref), (grid_hbm, gfull.at[:, mine]), (we_hbm, wef.at[:, mine]),
                (mesh_hbm, mesh_ref), (wp_hbm, wpf.at[:, mine]), (wd_hbm, wdf.at[:, mine]),
            )
        )
    ]
    for copy in loads:
        copy.start()
    barrier = pltpu.get_barrier_semaphore()
    for d in range(1, bands):
        pl.semaphore_signal(
            barrier, inc=1, device_id=band_at(lax.rem(b + d, bands)),
            device_id_type=pl.DeviceIdType.MESH,
        )
    pl.semaphore_signal(
        barrier, inc=1, device_id={"feat": 1 - f}, device_id_type=pl.DeviceIdType.MESH
    )

    def slots(raw):
        inner = raw & (shard - 1)
        home_id = (inner >> (home.bit_length() - 1)) * n_mesh + (raw >> (shard.bit_length() - 1))
        return (home_id - b + 1) * home + (inner & (home - 1))

    order = lax.broadcasted_iota(jnp.int32, dst_ref.shape, 0)
    enc_ids = jnp.where(order < count_ref[...], slots(dst_ref[...]), -1)
    dec_ids = slots(src_ref[...])
    idt[...] = jnp.concatenate([enc_ids, enc_ids], axis=0).astype(F32).T
    stage[0:KP, :] = pi_ref[...]
    stage[KP:8, :] = jnp.zeros((8 - KP, shard), jnp.int32)

    def one_hot(target, ids):
        step = 64
        for r in range(0, win, step):
            node = lax.broadcasted_iota(jnp.int32, (step, rows), 0) + r
            acc = jnp.zeros((step, rows), F32)
            for k in range(ids.shape[0]):
                acc = acc + jnp.where(node == ids[k:k + 1, :], 1.0, 0.0)
            target[r:r + step, :] = acc.astype(BF)

    one_hot(dec_m, dec_ids)
    loads[0].wait()
    dec_win = mm(dec_m[...], cot_ref[...]) / KD
    halo_out[0] = dec_win[2 * home:, :].astype(BF)
    halo_out[1] = dec_win[:home, :].astype(BF)
    own_win[0] = dec_win[home:2 * home, :]
    one_hot(enc_m, enc_ids)
    psall[m] = stage[...]

    @pl.when(b == 0)
    def _():
        halo_in[0] = jnp.zeros((home, half), BF)
        halo_in[2] = jnp.zeros((home, half), BF)

    @pl.when(b == bands - 1)
    def _():
        halo_in[1] = jnp.zeros((home, half), BF)
        halo_in[3] = jnp.zeros((home, half), BF)

    for copy in loads[1:]:
        copy.wait()
    pl.semaphore_wait(barrier, bands)

    wides = [
        remote(t.at[:, mine], t.at[:, mine], s_f.at[i], r_f.at[i], feat=1 - f)
        for i, t in enumerate((gfull, wef, wpf, wdf))
    ]
    indices = [
        remote(stage, psall.at[m], s_p.at[e - 1], r_p.at[e - 1], mesh=lax.rem(m + e, n_mesh))
        for e in range(1, n_mesh)
    ]
    wides[0].start()

    def halo(i, up):
        slot = 2 * i + (0 if up else 1)
        return remote(
            halo_out.at[slot], halo_in.at[slot], s_h.at[slot], r_h.at[slot],
            **band_at(b + 1 if up else b - 1),
        )

    def halo_start(i):
        @pl.when(b < bands - 1)
        def _():
            halo(i, True).start()

        @pl.when(b > 0)
        def _():
            halo(i, False).start()

    def halo_recv(i):
        @pl.when(b > 0)
        def _():
            halo(i, True).wait_recv()

        @pl.when(b < bands - 1)
        def _():
            halo(i, False).wait_recv()

    def halo_sent(i):
        @pl.when(b < bands - 1)
        def _():
            halo(i, True).wait_send()

        @pl.when(b > 0)
        def _():
            halo(i, False).wait_send()

    halo_start(0)
    for copy in indices:
        copy.start()

    wides[0].wait_recv()
    for copy in wides[1:]:
        copy.start()
    pre = mm(gfull[...], wef[:, mine])
    enc_win = mm(enc_m[...], (pre * sigm(pre)).astype(BF)) * factor
    halo_out[2] = enc_win[2 * home:, :].astype(BF)
    halo_out[3] = enc_win[:home, :].astype(BF)
    own_win[1] = enc_win[home:2 * home, :]
    halo_start(1)

    for copy in indices:
        copy.wait_recv()
    step = 64
    for i in range(n_mesh):
        pst[i * shard:(i + 1) * shard, :] = psall[i].astype(F32).T

    def build_a(t, carry):
        r = pl.multiple_of(t * step, step)
        node = lax.broadcasted_iota(jnp.int32, (step, nodes), 1).astype(F32)
        acc = jnp.zeros((step, nodes), F32)
        for k in range(KP):
            acc = acc + jnp.where(node == pst[pl.ds(r, step), k:k + 1], 1.0, 0.0)
        inc_a[pl.ds(r, step), :] = acc.astype(BF)
        return carry

    def build_t(t, carry):
        r = pl.multiple_of(t * step, step)
        for i in range(n_mesh):
            node = lax.broadcasted_iota(jnp.int32, (step, shard), 0) + r
            acc = jnp.zeros((step, shard), F32)
            for k in range(KP):
                acc = acc + jnp.where(node == psall[i, k:k + 1, :], 1.0, 0.0)
            inc_t[pl.ds(r, step), i * shard:(i + 1) * shard] = acc.astype(BF)
        return carry

    def build_e(t, carry):
        r = pl.multiple_of(t * step, step)
        node = lax.broadcasted_iota(jnp.int32, (step, win), 1).astype(F32)
        acc = jnp.zeros((step, win), F32)
        for k in range(KE):
            acc = acc + jnp.where(node == idt[pl.ds(r, step), k:k + 1], 1.0, 0.0)
        enc_t[pl.ds(r, step), :] = acc.astype(BF)
        return carry

    def block(array, d, e):
        at_l = lax.rem(l + n_lat - d, n_lat)
        at_m = lax.rem(m + n_mesh - e, n_mesh)
        return array.at[pl.ds(pl.multiple_of(at_m * shard + at_l * home, home), home), mine]

    def along_lat(array, a, d):
        own = block(array, 0, 0)
        return remote(own, own, s_z.at[a, d - 1], r_z.at[a, d - 1], lat=lax.rem(l + d, n_lat))

    def recv_lat(array, a, d):
        view = block(array, d, 0)
        return remote(view, view, s_z.at[a, d - 1], r_z.at[a, d - 1], lat=lax.rem(l + d, n_lat))

    def along_mesh(array, a, d, e):
        view = block(array, d, 0)
        return remote(
            view, view, s_x.at[a, d, e - 1], r_x.at[a, d, e - 1], mesh=lax.rem(m + e, n_mesh)
        )

    def recv_mesh(array, a, d, e):
        view = block(array, d, e)
        return remote(
            view, view, s_x.at[a, d, e - 1], r_x.at[a, d, e - 1], mesh=lax.rem(m + e, n_mesh)
        )

    def along_feat(array, a, d, e):
        view = block(array, d, e)
        return remote(view, view, s_c.at[a, d, e], r_c.at[a, d, e], feat=1 - f)

    def spread_own(array, a):
        for e in range(1, n_mesh):
            along_mesh(array, a, 0, e).start()
        for d in range(1, n_lat):
            along_lat(array, a, d).start()
        along_feat(array, a, 0, 0).start()

    def spread_lat(array, a):
        for d in range(1, n_lat):
            recv_lat(array, a, d).wait_recv()
            for e in range(1, n_mesh):
                along_mesh(array, a, d, e).start()
            along_feat(array, a, d, 0).start()

    def spread_mesh(array, a):
        for d in range(n_lat):
            for e in range(1, n_mesh):
                recv_mesh(array, a, d, e).wait_recv()
                along_feat(array, a, d, e).start()

    def spread_done(array, a):
        for d in range(n_lat):
            for e in range(n_mesh):
                along_feat(array, a, d, e).wait_recv()

    def spread_sent(array, a):
        for d in range(1, n_lat):
            along_lat(array, a, d).wait_send()
        for d in range(n_lat):
            for e in range(n_mesh):
                if e:
                    along_mesh(array, a, d, e).wait_send()
                along_feat(array, a, d, e).wait_send()

    def banded(i):
        return own_win[i] + halo_in[2 * i].astype(F32) + halo_in[2 * i + 1].astype(F32)

    home_rows = pl.ds(pl.multiple_of(m * shard + l * home, home), home)
    halo_recv(0)
    ddec[home_rows, mine] = banded(0).astype(BF)
    spread_own(ddec, 1)
    lax.fori_loop(0, rows // step, build_e, 0)
    halo_recv(1)
    mesh_home = mesh_ref[pl.ds(pl.multiple_of(l * home, home), home), :].astype(F32)
    one[home_rows, mine] = (mesh_home + banded(1)).astype(BF)
    spread_own(one, 0)
    lax.fori_loop(0, nodes // step, build_a, 0)
    spread_lat(one, 0)
    spread_lat(ddec, 1)
    spread_mesh(one, 0)
    lax.fori_loop(0, nodes // step, build_t, 0)
    wides[1].wait_recv()
    wides[2].wait_recv()
    wides[3].wait_recv()
    tile = min(512, nodes)
    spread_done(one, 0)

    def tiles(body):
        for r in range(0, nodes, tile):
            body(slice(r, r + tile))

    def proc(at):
        value = mm(one[at, :], wpf[...])
        sig = sigm(value)
        pmsg[at, :] = (value * sig).astype(BF)
        sg_proc[at, :] = sig * (1.0 + value * (1.0 - sig))

    tiles(proc)
    spread_mesh(ddec, 1)

    def second(at):
        total = mm(inc_a[at, :], pmsg[...])
        two[at, :] = (one[at, :].astype(F32) + total * (1.0 / KP)).astype(BF)

    tiles(second)

    pre_all = mm(gfull[...], wef[...])
    sig_all = sigm(pre_all)
    sg_enc[...] = sig_all * (1.0 + pre_all * (1.0 - sig_all))
    spread_done(ddec, 1)

    def decode(at):
        value = mm(two[at, :], wdf[...])
        sig = sigm(value)
        grad = sig * (1.0 + value * (1.0 - sig))
        dpd[at, :] = (ddec[at, :].astype(F32) * grad).astype(BF)
        back = mm(dpd[at, :], wdf[...], NT)
        dtwo[at, :] = back
        dtwo_b[at, :] = back.astype(BF)

    tiles(decode)

    def third(at):
        total = mm(inc_t[at, :], dtwo_b[...]) * (1.0 / KP)
        dpp[at, :] = (total * sg_proc[at, :]).astype(BF)
        gmesh[at, :] = (dtwo[at, :] + mm(dpp[at, :], wpf[...], NT)).astype(BF)

    tiles(third)

    def store(i, source, target):
        copy = pltpu.make_async_copy(source, target, s_out.at[i])
        copy.start()
        return copy

    own_rows = pl.ds(pl.multiple_of(m * shard, shard), shard)
    stores = [store(0, gmesh.at[own_rows, mine], gm_hbm)]
    for j in range(3):
        at = jnp.clip(b + j - 1, 0, bands - 1)
        first = pl.multiple_of(lax.rem(at, n_mesh) * shard + at // n_mesh * home, home)
        dwin[j * home:(j + 1) * home, :] = gmesh[pl.ds(first, home), :]
    dpe[...] = (mm(enc_t[...], dwin[...]) * factor * sg_enc[...]).astype(BF)
    weight = mm(gfull[...], dpe[:, mine], TN)
    rs_own[...] = weight
    rs_src[...] = weight.astype(BF)

    def part(at_l, at_m):
        return pl.ds(pl.multiple_of((at_m * n_lat + at_l) * chunk, chunk), chunk)

    def ahead(d):
        return lax.rem(l + d, n_lat)

    def behind(d):
        return lax.rem(l + n_lat - d, n_lat)

    def across(d, e):
        to = lax.rem(m + e, n_mesh)
        return remote(
            rs_src.at[part(ahead(d), to), :], rs_x.at[d, e - 1], s_rx.at[d, e - 1],
            r_rx.at[d, e - 1], mesh=to,
        )

    pieces = list(range(1, n_lat)) + [0]
    crossing = {(d, e): across(d, e) for d in pieces for e in range(1, n_mesh)}
    for copy in crossing.values():
        copy.start()
    gwd_ref[...] = mm(two[...], dpd[:, mine], TN).astype(BF)
    stores.append(store(1, gwd_ref, gwd_hbm))

    def column_sum(d):
        total = rs_own[part(ahead(d), m), :]
        for e in range(1, n_mesh):
            crossing[d, e].wait_recv()
            total = total + rs_x[d, e - 1].astype(F32)
        return total

    scatter, gather = [], []
    for d in range(1, n_lat):
        rs_out[d - 1] = column_sum(d).astype(BF)
        scatter.append(
            remote(
                rs_out.at[d - 1], rs_in.at[d - 1], s_rs.at[d - 1], r_rs.at[d - 1], lat=ahead(d)
            )
        )
        scatter[-1].start()
    gwp_ref[...] = mm(one[...], dpp[:, mine], TN).astype(BF)
    stores.append(store(2, gwp_ref, gwp_hbm))
    total = column_sum(0)
    for d in range(1, n_lat):
        scatter[d - 1].wait_recv()
        total = total + rs_in[d - 1].astype(F32)
    ag[part(l, m), :] = total.astype(BF)

    def ag_lat(d, view):
        return remote(view, view, s_ag.at[d - 1], r_ag.at[d - 1], lat=ahead(d))

    def ag_mesh(d, e, view):
        return remote(
            view, view, s_ax.at[d, e - 1], r_ax.at[d, e - 1], mesh=lax.rem(m + e, n_mesh)
        )

    own_part = ag.at[part(l, m), :]
    for d in range(1, n_lat):
        gather.append(ag_lat(d, own_part))
    for e in range(1, n_mesh):
        gather.append(ag_mesh(0, e, own_part))
    for copy in gather:
        copy.start()
    terms = mm(dpe[...], wef[mine, :], NT)
    gg_ref[...] = (cot_ref[...].astype(F32) + terms).astype(BF)
    stores.append(store(3, gg_ref, gg_hbm))
    for d in range(1, n_lat):
        view = ag.at[part(behind(d), m), :]
        ag_lat(d, view).wait_recv()
        for e in range(1, n_mesh):
            gather.append(ag_mesh(d, e, view))
            gather[-1].start()
    for copy in wides + indices:
        copy.wait_send()
    halo_sent(0)
    halo_sent(1)
    spread_sent(one, 0)
    spread_sent(ddec, 1)
    for copy in list(crossing.values()) + scatter:
        copy.wait_send()
    for d in range(n_lat):
        for e in range(1, n_mesh):
            at_m = lax.rem(m + n_mesh - e, n_mesh)
            ag_mesh(d, e, ag.at[part(behind(d), at_m), :]).wait_recv()
    stores.append(store(4, ag, gwe_hbm))
    for copy in gather:
        copy.wait_send()
    for copy in stores:
        copy.wait()


def widen_kernel(*refs):
    for source, target in zip(refs[:5], refs[5:]):
        target[...] = source[...].astype(target.dtype)


def local_fused(
    grid_in, mesh_in, w_enc, w_proc, w_dec, enc_dst, enc_count, dec_src, proc_src, cotangent
):
    n_mesh = lax.axis_size("mesh")
    n_lat = lax.axis_size("lat")
    rows, half = grid_in.shape
    shard = mesh_in.shape[0]
    wide = 2 * half
    home = shard // n_lat
    bands = n_lat * n_mesh
    nodes = shard * n_mesh
    win = 3 * home
    v = pltpu.VMEM
    dma = pltpu.SemaphoreType.DMA
    vmem = pl.BlockSpec(memory_space=pltpu.VMEM)
    hbm = pl.BlockSpec(memory_space=pl.ANY)
    shaped = jax.ShapeDtypeStruct
    parts = pl.pallas_call(
        functools.partial(fused_kernel, n_lat, n_mesh),
        out_shape=(
            shaped((rows, half), BF),
            shaped((shard, half), BF),
            shaped((wide, half), BF),
            shaped((wide, half), BF),
            shaped((wide, half), BF),
        ),
        in_specs=[hbm] * 5 + [vmem] * 4 + [hbm],
        out_specs=(hbm,) * 5,
        scratch_shapes=[
            v((shard, half), BF), v((rows, half), BF), v((rows, half), BF), v((wide, half), BF),
            v((wide, half), BF), dma((6,)), dma((5,)),
            v((rows, wide), BF), v((wide, wide), BF), v((wide, wide), BF), v((wide, wide), BF),
            v((8, shard), jnp.int32), v((n_mesh, 8, shard), jnp.int32), v((nodes, 8), F32), v((rows, 8), F32),
            v((win, rows), BF), v((rows, win), BF), v((win, rows), BF),
            v((nodes, nodes), BF), v((nodes, nodes), BF),
            v((4, home, half), BF), v((4, home, half), BF), v((2, home, half), F32),
            v((rows, wide), F32),
            v((nodes, wide), BF), v((nodes, wide), BF), v((nodes, wide), F32),
            v((nodes, wide), BF), v((nodes, wide), BF), v((nodes, wide), BF),
            v((nodes, wide), F32), v((nodes, wide), BF), v((nodes, wide), BF),
            v((nodes, wide), BF), v((rows, wide), BF), v((win, wide), BF),
            v((wide, half), BF), v((wide, half), F32),
            v((n_lat, n_mesh - 1, wide // bands, half), BF),
            v((n_lat - 1, wide // bands, half), BF), v((n_lat - 1, wide // bands, half), BF),
            v((wide, half), BF),
            dma((4,)), dma((4,)), dma((n_mesh - 1,)), dma((n_mesh - 1,)),
            dma((4,)), dma((4,)),
            dma((2, n_lat - 1)), dma((2, n_lat - 1)),
            dma((2, n_lat, n_mesh - 1)), dma((2, n_lat, n_mesh - 1)),
            dma((2, n_lat, n_mesh)), dma((2, n_lat, n_mesh)),
            dma((n_lat, n_mesh - 1)), dma((n_lat, n_mesh - 1)),
            dma((n_lat - 1,)), dma((n_lat - 1,)), dma((n_lat - 1,)), dma((n_lat - 1,)),
            dma((n_lat, n_mesh - 1)), dma((n_lat, n_mesh - 1)),
        ],
        compiler_params=pltpu.CompilerParams(
            collective_id=0, has_side_effects=True, vmem_limit_bytes=56 * 1024 * 1024
        ),
        cost_estimate=pl.CostEstimate(
            flops=10 * nodes * wide * wide, bytes_accessed=8 * rows * wide,
            transcendentals=4 * nodes * wide,
        ),
    )(grid_in, mesh_in, w_enc, w_proc, w_dec, enc_dst.T, enc_count[None, :], dec_src.T, proc_src.T, cotangent)
    return tuple(pl.pallas_call(
        widen_kernel,
        out_shape=(
            shaped((rows, half), BF),
            shaped((shard, half), BF),
            shaped((wide, half), F32),
            shaped((wide, half), F32),
            shaped((wide, half), F32),
        ),
        in_specs=[vmem] * 5,
        out_specs=(vmem,) * 5,
        compiler_params=pltpu.CompilerParams(vmem_limit_bytes=60 * 1024 * 1024),
    )(*parts))


def solution(mesh):
    bands = mesh.shape["lat"] * mesh.shape["mesh"]
    body = local_fused if bands <= 8 and mesh.shape["feat"] == 2 else local_staged
    placed = (
        P(("groups", "lat", "mesh"), "feat"),
        P(("groups", "mesh"), "feat"),
        P(None, "feat"),
        P(None, "feat"),
        P(None, "feat"),
        P(("groups", "lat", "mesh"), None),
        P(("groups", "lat", "mesh")),
        P(("groups", "lat", "mesh"), None),
        P(("groups", "mesh"), None),
        P(("groups", "lat", "mesh"), "feat"),
    )
    return jax.shard_map(
        body,
        mesh=mesh,
        in_specs=placed,
        out_specs=(
            P(("groups", "lat", "mesh"), "feat"),
            P(("groups", "mesh"), "feat"),
            P("groups", "feat"),
            P("groups", "feat"),
            P("groups", "feat"),
        ),
        check_vma=False,
    )
```

```python
import functools

import jax
import jax.numpy as jnp
from jax import lax
from jax.experimental import pallas as pl
from jax.experimental.pallas import tpu as pltpu
from jax.sharding import PartitionSpec as P

KE = 4
KD = 3
KP = 6


def with_halo(value, sides, width):
    for axis, dim in sides:
        size, length = (lax.axis_size(axis), value.shape[dim])
        up = [(i, (i + 1) % size) for i in range(size - 1)]
        down = [(j, i) for i, j in up]
        last = lax.slice_in_dim(value, length - width, length, axis=dim)
        first = lax.slice_in_dim(value, 0, width, axis=dim)
        before = lax.ppermute(last, axis, up)
        after = lax.ppermute(first, axis, down)
        value = jnp.concatenate([before, value, after], axis=dim)
    return value


def silu_grad(pre):
    sig = jax.nn.sigmoid(pre)
    return sig * (1.0 + pre * (1.0 - sig))


def window_slots(targets, is_valid, shard_rows, home_rows, n_mesh, band_index):
    owner_shard = targets // shard_rows
    inner_row = targets % shard_rows
    home_id = inner_row // home_rows * n_mesh + owner_shard
    slot_ids = (home_id - band_index + 1) * home_rows + inner_row % home_rows
    return jnp.where(is_valid, slot_ids, -1)


def window_matrix(slot_ids, win_rows):
    row_ids = jnp.arange(win_rows, dtype=jnp.int32)[:, None]
    matrix = jnp.zeros((win_rows, slot_ids.shape[0]), jnp.bfloat16)
    for column in range(slot_ids.shape[1]):
        matrix = matrix + (row_ids == slot_ids[:, column][None, :]).astype(jnp.bfloat16)
    return matrix


def band_sum(window, home_rows):
    stacked = window.reshape(3, home_rows, window.shape[1])
    padded_win = with_halo(stacked.astype(jnp.bfloat16), ((("lat", "mesh"), 0),), 3).astype(
        stacked.dtype
    )
    return padded_win[2] + padded_win[4] + padded_win[6]


def collect_rows(home_block):
    return lax.all_gather(home_block, "lat", axis=0, tiled=True)


def widen(latent):
    return lax.all_gather(latent, "feat", axis=1, tiled=True)


def back_product(d_pre, weight):
    return lax.dot_general(
        d_pre, weight, (((1,), (1,)), ((), ())), preferred_element_type=jnp.float32
    )


def mesh_back(d_pre, weight):
    return lax.psum_scatter(
        back_product(d_pre, weight).astype(jnp.bfloat16), "feat", scatter_dimension=1, tiled=True
    ).astype(jnp.float32)


def contract_rows(left_rows, right_rows):
    return lax.dot_general(
        left_rows, right_rows, (((0,), (0,)), ((), ())), preferred_element_type=jnp.float32
    )


def local_staged(grid_in, mesh_in, w_enc, w_proc, w_dec, enc_dst, enc_count, dec_src, proc_src, cotangent):
    n_mesh = lax.axis_size("mesh")
    n_lat = lax.axis_size("lat")
    shard_rows = mesh_in.shape[0]
    home_rows = shard_rows // n_lat
    grid_rows = grid_in.shape[0]
    enc_factor = home_rows / grid_rows
    band_index = lax.axis_index("lat") * n_mesh + lax.axis_index("mesh")
    home_first = lax.axis_index("lat") * home_rows
    win_rows = 3 * home_rows
    enc_valid = jnp.arange(KE, dtype=jnp.int32)[None, :] < enc_count[:, None]
    enc_matrix = window_matrix(
        window_slots(enc_dst, enc_valid, shard_rows, home_rows, n_mesh, band_index), win_rows
    )
    dec_valid = jnp.ones(dec_src.shape, jnp.bool_)
    dec_matrix = window_matrix(
        window_slots(dec_src, dec_valid, shard_rows, home_rows, n_mesh, band_index), win_rows
    )
    grid_full = lax.all_gather(grid_in, "feat", axis=1, tiled=True)
    pre_enc = jnp.dot(grid_full, w_enc, preferred_element_type=jnp.float32)
    enc_msg = jax.nn.silu(pre_enc).astype(jnp.bfloat16)
    enc_window = jnp.dot(enc_matrix, enc_msg, preferred_element_type=jnp.float32) * enc_factor
    aggregate_home = band_sum(enc_window, home_rows)
    mesh_home = lax.dynamic_slice_in_dim(mesh_in, home_first, home_rows, 0)
    latent_one = collect_rows((mesh_home.astype(jnp.float32) + aggregate_home).astype(jnp.bfloat16))
    one_full = widen(latent_one)
    pre_proc = jnp.dot(one_full, w_proc, preferred_element_type=jnp.float32)
    proc_msg = jax.nn.silu(pre_proc).astype(jnp.bfloat16)

    def incidence(row_count):
        node_ids = jnp.arange(row_count, dtype=jnp.int32)
        matrix = jnp.zeros((shard_rows, row_count), jnp.bfloat16)
        for column in range(KP):
            matrix = matrix + (proc_src[:, column][:, None] == node_ids[None, :]).astype(
                jnp.bfloat16
            )
        return matrix

    shard_piece = lax.all_gather(proc_msg, "mesh", axis=0, tiled=True)
    neighbour_sum = jnp.dot(
        incidence(shard_piece.shape[0]), shard_piece, preferred_element_type=jnp.float32
    )
    latent_two = (latent_one.astype(jnp.float32) + neighbour_sum / KP).astype(jnp.bfloat16)
    two_full = widen(latent_two)
    pre_dec = jnp.dot(two_full, w_dec, preferred_element_type=jnp.float32)
    dec_window = jnp.dot(dec_matrix, cotangent, preferred_element_type=jnp.float32) / KD
    d_dec = collect_rows(band_sum(dec_window, home_rows).astype(jnp.bfloat16))
    d_pre_dec = (d_dec.astype(jnp.float32) * silu_grad(pre_dec)).astype(jnp.bfloat16)
    d_two = mesh_back(d_pre_dec, w_dec)
    d_two_b = d_two.astype(jnp.bfloat16)
    d_proc = (
        lax.psum_scatter(
            contract_rows(incidence(shard_rows * lax.axis_size("mesh")), d_two_b).astype(
                jnp.bfloat16
            ),
            "mesh",
            scatter_dimension=0,
            tiled=True,
        ).astype(jnp.float32)
        / KP
    )
    d_pre_proc = (d_proc * silu_grad(pre_proc)).astype(jnp.bfloat16)
    d_one = d_two + mesh_back(d_pre_proc, w_proc)
    grad_mesh = d_one.astype(jnp.bfloat16)
    grad_home = lax.dynamic_slice_in_dim(grad_mesh, home_first, home_rows, 0)
    mesh_window = with_halo(grad_home, ((("lat", "mesh"), 0),), home_rows)
    d_enc = contract_rows(enc_matrix, mesh_window) * enc_factor
    d_pre_enc = (d_enc * silu_grad(pre_enc)).astype(jnp.bfloat16)
    grid_terms = lax.psum_scatter(
        back_product(d_pre_enc, w_enc).astype(jnp.bfloat16), "feat", scatter_dimension=1, tiled=True
    ).astype(jnp.float32)
    grad_grid = (cotangent.astype(jnp.float32) + grid_terms).astype(jnp.bfloat16)
    enc_term = contract_rows(grid_full, d_pre_enc)
    grad_w_proc, grad_w_dec = (
        lax.psum(contract_rows(one_full, d_pre_proc).astype(jnp.bfloat16), "mesh").astype(
            jnp.float32
        ),
        lax.psum(contract_rows(two_full, d_pre_dec).astype(jnp.bfloat16), "mesh").astype(
            jnp.float32
        ),
    )
    grad_w_enc = lax.psum(enc_term, ("lat", "mesh"))
    return (grad_grid, grad_mesh, grad_w_enc, grad_w_proc, grad_w_dec)


BF = jnp.bfloat16
F32 = jnp.float32
NN = (((1,), (0,)), ((), ()))
NT = (((1,), (1,)), ((), ()))
TN = (((0,), (0,)), ((), ()))


def mm(left, right, dims=NN):
    return lax.dot_general(left, right, dims, preferred_element_type=F32)


def sigm(value):
    return 1.0 / (1.0 + jnp.exp(-value))


def fused_kernel(
    n_lat, n_mesh,
    grid_hbm, mesh_hbm, we_hbm, wp_hbm, wd_hbm, dst_ref, count_ref, src_ref, pi_ref, cot_hbm,
    gg_hbm, gm_hbm, gwe_hbm, gwp_hbm, gwd_hbm,
    mesh_ref, cot_ref, gg_ref, gwp_ref, gwd_ref, s_in, s_out,
    grid_t, gfull, wef, wpf, wdf, stage, psall, pst, idt, enc_m, enc_t, dec_m, inc_a, inc_t,
    halo_out, halo_in, own_win, sg_enc, one, ddec, sg_proc, pmsg, two, dpd, dtwo, dtwo_b, dpp,
    gmesh, dpe, dwin, rs_src, rs_own, rs_in, ag,
    s_f, r_f, s_p, r_p, s_h, r_h, s_z, r_z, s_x, r_x, s_c, r_c, s_rs, r_rs, s_ag, r_ag,
):
    rows, half = cot_ref.shape
    shard = mesh_ref.shape[0]
    home = shard // n_lat
    bands = n_lat * n_mesh
    nodes = shard * n_mesh
    wide = 2 * half
    chunk = wide // bands
    win = 3 * home
    factor = home / rows
    l = lax.axis_index("lat")
    m = lax.axis_index("mesh")
    f = lax.axis_index("feat")
    b = l * n_mesh + m
    mine = pl.ds(pl.multiple_of(f * half, half), half)

    def remote(source, target, send, recv, **where):
        return pltpu.make_async_remote_copy(
            src_ref=source, dst_ref=target, send_sem=send, recv_sem=recv,
            device_id=where, device_id_type=pl.DeviceIdType.MESH,
        )

    def band_at(index):
        return {"lat": index // n_mesh, "mesh": lax.rem(index, n_mesh)}

    loads = [
        pltpu.make_async_copy(s, t, s_in.at[i])
        for i, (s, t) in enumerate(
            (
                (cot_hbm, cot_ref), (grid_hbm, gfull.at[:, mine]), (we_hbm, wef.at[:, mine]),
                (mesh_hbm, mesh_ref), (wp_hbm, wpf.at[:, mine]), (wd_hbm, wdf.at[:, mine]),
            )
        )
    ]
    for copy in loads:
        copy.start()
    barrier = pltpu.get_barrier_semaphore()
    for d in range(1, bands):
        pl.semaphore_signal(
            barrier, inc=1, device_id=band_at(lax.rem(b + d, bands)),
            device_id_type=pl.DeviceIdType.MESH,
        )
    pl.semaphore_signal(
        barrier, inc=1, device_id={"feat": 1 - f}, device_id_type=pl.DeviceIdType.MESH
    )

    def slots(raw):
        inner = raw & (shard - 1)
        home_id = (inner >> (home.bit_length() - 1)) * n_mesh + (raw >> (shard.bit_length() - 1))
        return (home_id - b + 1) * home + (inner & (home - 1))

    order = lax.broadcasted_iota(jnp.int32, dst_ref.shape, 0)
    enc_ids = jnp.where(order < count_ref[...], slots(dst_ref[...]), -1)
    dec_ids = slots(src_ref[...])
    idt[...] = jnp.concatenate([enc_ids, enc_ids], axis=0).astype(F32).T
    stage[0:KP, :] = pi_ref[...]
    stage[KP:8, :] = jnp.zeros((8 - KP, shard), jnp.int32)

    def one_hot(target, ids):
        step = 64
        for r in range(0, win, step):
            node = lax.broadcasted_iota(jnp.int32, (step, rows), 0) + r
            acc = jnp.zeros((step, rows), F32)
            for k in range(ids.shape[0]):
                acc = acc + jnp.where(node == ids[k:k + 1, :], 1.0, 0.0)
            target[r:r + step, :] = acc.astype(BF)

    one_hot(dec_m, dec_ids)
    loads[0].wait()
    dec_win = mm(dec_m[...], cot_ref[...]) / KD
    halo_out[0] = dec_win[2 * home:, :].astype(BF)
    halo_out[1] = dec_win[:home, :].astype(BF)
    own_win[0] = dec_win[home:2 * home, :]
    one_hot(enc_m, enc_ids)
    psall[m] = stage[...]

    @pl.when(b == 0)
    def _():
        halo_in[0] = jnp.zeros((home, half), BF)
        halo_in[2] = jnp.zeros((home, half), BF)

    @pl.when(b == bands - 1)
    def _():
        halo_in[1] = jnp.zeros((home, half), BF)
        halo_in[3] = jnp.zeros((home, half), BF)

    for copy in loads[1:]:
        copy.wait()
    pl.semaphore_wait(barrier, bands)

    wides = [
        remote(t.at[:, mine], t.at[:, mine], s_f.at[i], r_f.at[i], feat=1 - f)
        for i, t in enumerate((gfull, wef, wpf, wdf))
    ]
    indices = [
        remote(stage, psall.at[m], s_p.at[e - 1], r_p.at[e - 1], mesh=lax.rem(m + e, n_mesh))
        for e in range(1, n_mesh)
    ]
    wides[0].start()

    def halo(i, up):
        slot = 2 * i + (0 if up else 1)
        return remote(
            halo_out.at[slot], halo_in.at[slot], s_h.at[slot], r_h.at[slot],
            **band_at(b + 1 if up else b - 1),
        )

    def halo_start(i):
        @pl.when(b < bands - 1)
        def _():
            halo(i, True).start()

        @pl.when(b > 0)
        def _():
            halo(i, False).start()

    def halo_recv(i):
        @pl.when(b > 0)
        def _():
            halo(i, True).wait_recv()

        @pl.when(b < bands - 1)
        def _():
            halo(i, False).wait_recv()

    def halo_sent(i):
        @pl.when(b < bands - 1)
        def _():
            halo(i, True).wait_send()

        @pl.when(b > 0)
        def _():
            halo(i, False).wait_send()

    halo_start(0)
    for copy in indices:
        copy.start()

    wides[0].wait_recv()
    for copy in wides[1:]:
        copy.start()
    pre = mm(gfull[...], wef[:, mine])
    enc_win = mm(enc_m[...], (pre * sigm(pre)).astype(BF)) * factor
    halo_out[2] = enc_win[2 * home:, :].astype(BF)
    halo_out[3] = enc_win[:home, :].astype(BF)
    own_win[1] = enc_win[home:2 * home, :]
    halo_start(1)

    for copy in indices:
        copy.wait_recv()
    step = 64
    for i in range(n_mesh):
        pst[i * shard:(i + 1) * shard, :] = psall[i].astype(F32).T

    def build_a(t, carry):
        r = pl.multiple_of(t * step, step)
        node = lax.broadcasted_iota(jnp.int32, (step, nodes), 1).astype(F32)
        acc = jnp.zeros((step, nodes), F32)
        for k in range(KP):
            acc = acc + jnp.where(node == pst[pl.ds(r, step), k:k + 1], 1.0, 0.0)
        inc_a[pl.ds(r, step), :] = acc.astype(BF)
        return carry

    def build_t(t, carry):
        r = pl.multiple_of(t * step, step)
        for i in range(n_mesh):
            node = lax.broadcasted_iota(jnp.int32, (step, shard), 0) + r
            acc = jnp.zeros((step, shard), F32)
            for k in range(KP):
                acc = acc + jnp.where(node == psall[i, k:k + 1, :], 1.0, 0.0)
            inc_t[pl.ds(r, step), i * shard:(i + 1) * shard] = acc.astype(BF)
        return carry

    def build_e(t, carry):
        r = pl.multiple_of(t * step, step)
        node = lax.broadcasted_iota(jnp.int32, (step, win), 1).astype(F32)
        acc = jnp.zeros((step, win), F32)
        for k in range(KE):
            acc = acc + jnp.where(node == idt[pl.ds(r, step), k:k + 1], 1.0, 0.0)
        enc_t[pl.ds(r, step), :] = acc.astype(BF)
        return carry

    def block(array, d, e):
        at_l = lax.rem(l + n_lat - d, n_lat)
        at_m = lax.rem(m + n_mesh - e, n_mesh)
        return array.at[pl.ds(pl.multiple_of(at_m * shard + at_l * home, home), home), mine]

    def along_lat(array, a, d):
        own = block(array, 0, 0)
        return remote(own, own, s_z.at[a, d - 1], r_z.at[a, d - 1], lat=lax.rem(l + d, n_lat))

    def recv_lat(array, a, d):
        view = block(array, d, 0)
        return remote(view, view, s_z.at[a, d - 1], r_z.at[a, d - 1], lat=lax.rem(l + d, n_lat))

    def along_mesh(array, a, d, e):
        view = block(array, d, 0)
        return remote(
            view, view, s_x.at[a, d, e - 1], r_x.at[a, d, e - 1], mesh=lax.rem(m + e, n_mesh)
        )

    def recv_mesh(array, a, d, e):
        view = block(array, d, e)
        return remote(
            view, view, s_x.at[a, d, e - 1], r_x.at[a, d, e - 1], mesh=lax.rem(m + e, n_mesh)
        )

    def along_feat(array, a, d, e):
        view = block(array, d, e)
        return remote(view, view, s_c.at[a, d, e], r_c.at[a, d, e], feat=1 - f)

    def spread_own(array, a):
        for e in range(1, n_mesh):
            along_mesh(array, a, 0, e).start()
        for d in range(1, n_lat):
            along_lat(array, a, d).start()
        along_feat(array, a, 0, 0).start()

    def spread_lat(array, a):
        for d in range(1, n_lat):
            recv_lat(array, a, d).wait_recv()
            for e in range(1, n_mesh):
                along_mesh(array, a, d, e).start()
            along_feat(array, a, d, 0).start()

    def spread_mesh(array, a):
        for d in range(n_lat):
            for e in range(1, n_mesh):
                recv_mesh(array, a, d, e).wait_recv()
                along_feat(array, a, d, e).start()

    def spread_done(array, a):
        for d in range(n_lat):
            for e in range(n_mesh):
                along_feat(array, a, d, e).wait_recv()

    def spread_sent(array, a):
        for d in range(1, n_lat):
            along_lat(array, a, d).wait_send()
        for d in range(n_lat):
            for e in range(n_mesh):
                if e:
                    along_mesh(array, a, d, e).wait_send()
                along_feat(array, a, d, e).wait_send()

    def banded(i):
        return own_win[i] + halo_in[2 * i].astype(F32) + halo_in[2 * i + 1].astype(F32)

    home_rows = pl.ds(pl.multiple_of(m * shard + l * home, home), home)
    halo_recv(0)
    ddec[home_rows, mine] = banded(0).astype(BF)
    spread_own(ddec, 1)
    lax.fori_loop(0, rows // step, build_e, 0)
    halo_recv(1)
    mesh_home = mesh_ref[pl.ds(pl.multiple_of(l * home, home), home), :].astype(F32)
    one[home_rows, mine] = (mesh_home + banded(1)).astype(BF)
    spread_own(one, 0)
    lax.fori_loop(0, nodes // step, build_a, 0)
    spread_lat(one, 0)
    spread_lat(ddec, 1)
    spread_mesh(one, 0)
    lax.fori_loop(0, nodes // step, build_t, 0)
    grid_t[...] = gfull[...].T
    wides[1].wait_recv()
    wides[2].wait_recv()
    wides[3].wait_recv()
    tile = min(512, nodes)
    spread_done(one, 0)

    def tiles(body):
        for r in range(0, nodes, tile):
            body(slice(r, r + tile))

    def proc(at):
        value = mm(one[at, :], wpf[...])
        sig = sigm(value)
        pmsg[at, :] = (value * sig).astype(BF)
        sg_proc[at, :] = sig * (1.0 + value * (1.0 - sig))

    tiles(proc)
    spread_mesh(ddec, 1)

    def second(at):
        total = mm(inc_a[at, :], pmsg[...])
        two[at, :] = (one[at, :].astype(F32) + total * (1.0 / KP)).astype(BF)

    tiles(second)

    pre_all = mm(gfull[...], wef[...])
    sig_all = sigm(pre_all)
    sg_enc[...] = sig_all * (1.0 + pre_all * (1.0 - sig_all))
    spread_done(ddec, 1)

    def decode(at):
        value = mm(two[at, :], wdf[...])
        sig = sigm(value)
        grad = sig * (1.0 + value * (1.0 - sig))
        dpd[at, :] = (ddec[at, :].astype(F32) * grad).astype(BF)
        back = mm(dpd[at, :], wdf[...], NT)
        dtwo[at, :] = back
        dtwo_b[at, :] = back.astype(BF)

    tiles(decode)

    def third(at):
        total = mm(inc_t[at, :], dtwo_b[...]) * (1.0 / KP)
        dpp[at, :] = (total * sg_proc[at, :]).astype(BF)
        gmesh[at, :] = (dtwo[at, :] + mm(dpp[at, :], wpf[...], NT)).astype(BF)

    tiles(third)

    def store(i, source, target):
        copy = pltpu.make_async_copy(source, target, s_out.at[i])
        copy.start()
        return copy

    own_rows = pl.ds(pl.multiple_of(m * shard, shard), shard)
    stores = [store(0, gmesh.at[own_rows, mine], gm_hbm)]
    for j in range(3):
        at = jnp.clip(b + j - 1, 0, bands - 1)
        first = pl.multiple_of(lax.rem(at, n_mesh) * shard + at // n_mesh * home, home)
        dwin[j * home:(j + 1) * home, :] = gmesh[pl.ds(first, home), :]

    def encode(cols):
        total = mm(enc_t[...], dwin[:, cols]) * factor
        dpe[:, cols] = (total * sg_enc[:, cols]).astype(BF)

    encode(mine)
    weight = mm(grid_t[...], dpe[:, mine])
    rs_own[...] = weight
    rs_src[...] = weight.astype(BF)

    def part(index):
        return pl.ds(pl.multiple_of(index * chunk, chunk), chunk)

    scatter, gather = [], []
    for d in range(1, bands):
        to = lax.rem(b + d, bands)
        scatter.append(
            remote(
                rs_src.at[part(to), :], rs_in.at[d - 1], s_rs.at[d - 1], r_rs.at[d - 1],
                **band_at(to),
            )
        )
        scatter[-1].start()
    encode(pl.ds(pl.multiple_of((1 - f) * half, half), half))
    gwd_ref[...] = mm(two[...], dpd[:, mine], TN).astype(BF)
    stores.append(store(1, gwd_ref, gwd_hbm))
    gwp_ref[...] = mm(one[...], dpp[:, mine], TN).astype(BF)
    stores.append(store(2, gwp_ref, gwp_hbm))
    total = rs_own[part(b), :]
    for d in range(1, bands):
        scatter[d - 1].wait_recv()
        total = total + rs_in[d - 1].astype(F32)
    ag[part(b), :] = total.astype(BF)
    for d in range(1, bands):
        gather.append(
            remote(
                ag.at[part(b), :], ag.at[part(b), :], s_ag.at[d - 1], r_ag.at[d - 1],
                **band_at(lax.rem(b + d, bands)),
            )
        )
        gather[-1].start()
    terms = mm(dpe[...], wef[mine, :], NT)
    gg_ref[...] = (cot_ref[...].astype(F32) + terms).astype(BF)
    stores.append(store(3, gg_ref, gg_hbm))
    for copy in wides + indices:
        copy.wait_send()
    halo_sent(0)
    halo_sent(1)
    spread_sent(one, 0)
    spread_sent(ddec, 1)
    for copy in scatter:
        copy.wait_send()
    for d in range(1, bands):
        view = ag.at[part(lax.rem(b + bands - d, bands)), :]
        remote(
            view, view, s_ag.at[d - 1], r_ag.at[d - 1], **band_at(lax.rem(b + d, bands))
        ).wait_recv()
    stores.append(store(4, ag, gwe_hbm))
    for copy in gather:
        copy.wait_send()
    for copy in stores:
        copy.wait()


def widen_kernel(*refs):
    for source, target in zip(refs[:5], refs[5:]):
        target[...] = source[...].astype(target.dtype)


def local_fused(
    grid_in, mesh_in, w_enc, w_proc, w_dec, enc_dst, enc_count, dec_src, proc_src, cotangent
):
    n_mesh = lax.axis_size("mesh")
    n_lat = lax.axis_size("lat")
    rows, half = grid_in.shape
    shard = mesh_in.shape[0]
    wide = 2 * half
    home = shard // n_lat
    bands = n_lat * n_mesh
    nodes = shard * n_mesh
    win = 3 * home
    v = pltpu.VMEM
    dma = pltpu.SemaphoreType.DMA
    vmem = pl.BlockSpec(memory_space=pltpu.VMEM)
    hbm = pl.BlockSpec(memory_space=pl.ANY)
    shaped = jax.ShapeDtypeStruct
    parts = pl.pallas_call(
        functools.partial(fused_kernel, n_lat, n_mesh),
        out_shape=(
            shaped((rows, half), BF),
            shaped((shard, half), BF),
            shaped((wide, half), BF),
            shaped((wide, half), BF),
            shaped((wide, half), BF),
        ),
        in_specs=[hbm] * 5 + [vmem] * 4 + [hbm],
        out_specs=(hbm,) * 5,
        scratch_shapes=[
            v((shard, half), BF), v((rows, half), BF), v((rows, half), BF), v((wide, half), BF),
            v((wide, half), BF), dma((6,)), dma((5,)),
            v((wide, rows), BF),
            v((rows, wide), BF), v((wide, wide), BF), v((wide, wide), BF), v((wide, wide), BF),
            v((8, shard), jnp.int32), v((n_mesh, 8, shard), jnp.int32), v((nodes, 8), F32), v((rows, 8), F32),
            v((win, rows), BF), v((rows, win), BF), v((win, rows), BF),
            v((nodes, nodes), BF), v((nodes, nodes), BF),
            v((4, home, half), BF), v((4, home, half), BF), v((2, home, half), F32),
            v((rows, wide), F32),
            v((nodes, wide), BF), v((nodes, wide), BF), v((nodes, wide), F32),
            v((nodes, wide), BF), v((nodes, wide), BF), v((nodes, wide), BF),
            v((nodes, wide), F32), v((nodes, wide), BF), v((nodes, wide), BF),
            v((nodes, wide), BF), v((rows, wide), BF), v((win, wide), BF),
            v((wide, half), BF), v((wide, half), F32),
            v((bands - 1, wide // bands, half), BF), v((wide, half), BF),
            dma((4,)), dma((4,)), dma((n_mesh - 1,)), dma((n_mesh - 1,)),
            dma((4,)), dma((4,)),
            dma((2, n_lat - 1)), dma((2, n_lat - 1)),
            dma((2, n_lat, n_mesh - 1)), dma((2, n_lat, n_mesh - 1)),
            dma((2, n_lat, n_mesh)), dma((2, n_lat, n_mesh)),
            dma((bands - 1,)), dma((bands - 1,)), dma((bands - 1,)), dma((bands - 1,)),
        ],
        compiler_params=pltpu.CompilerParams(
            collective_id=0, has_side_effects=True, vmem_limit_bytes=56 * 1024 * 1024
        ),
        cost_estimate=pl.CostEstimate(
            flops=10 * nodes * wide * wide, bytes_accessed=8 * rows * wide,
            transcendentals=4 * nodes * wide,
        ),
    )(grid_in, mesh_in, w_enc, w_proc, w_dec, enc_dst.T, enc_count[None, :], dec_src.T, proc_src.T, cotangent)
    sizes = (rows, shard, wide, wide, wide)
    return tuple(pl.pallas_call(
        widen_kernel,
        out_shape=(
            shaped((rows, half), BF),
            shaped((shard, half), BF),
            shaped((wide, half), F32),
            shaped((wide, half), F32),
            shaped((wide, half), F32),
        ),
        grid=(4,),
        in_specs=[pl.BlockSpec((r // 4, half), lambda i: (i, 0)) for r in sizes],
        out_specs=tuple(pl.BlockSpec((r // 4, half), lambda i: (i, 0)) for r in sizes),
        compiler_params=pltpu.CompilerParams(vmem_limit_bytes=60 * 1024 * 1024),
    )(*parts))


def solution(mesh):
    bands = mesh.shape["lat"] * mesh.shape["mesh"]
    body = local_fused if bands <= 8 and mesh.shape["feat"] == 2 else local_staged
    placed = (
        P(("groups", "lat", "mesh"), "feat"),
        P(("groups", "mesh"), "feat"),
        P(None, "feat"),
        P(None, "feat"),
        P(None, "feat"),
        P(("groups", "lat", "mesh"), None),
        P(("groups", "lat", "mesh")),
        P(("groups", "lat", "mesh"), None),
        P(("groups", "mesh"), None),
        P(("groups", "lat", "mesh"), "feat"),
    )
    return jax.shard_map(
        body,
        mesh=mesh,
        in_specs=placed,
        out_specs=(
            P(("groups", "lat", "mesh"), "feat"),
            P(("groups", "mesh"), "feat"),
            P("groups", "feat"),
            P("groups", "feat"),
            P("groups", "feat"),
        ),
        check_vma=False,
    )
```
